128 devices in a mesh: trip: 8 (over z_hi, y), slab: 16 (over z_lo, x, core).
Axes of the slice: x: 4, y: 4, z: 4 (z_hi: 2, z_lo: 2; z = z_hi * 2 + z_lo), core: 2. Of those that a mesh axis runs over, the one named last changes fastest.
Arguments:
- integrals: float32 [32, 256, 256, 256], P('trip', 'slab'), may hold values from -0.24 to 0.24
- amplitudes: float32 [32, 32, 256, 256], P('trip', 'slab'), may hold values from -6 to 6
- occ_energy: float32 [32], replicated, may hold values from -3 to -1
- vir_energy: float32 [256], replicated, may hold values from 0.5 to 3
- owner: int32 [32], replicated, may hold values from 0 to 7, as said below
- triples: int32 [2, 8, 3], replicated, may hold values from 0 to 31, as said below
Outputs:
- residual: float32 [32, 32, 256, 256], P('trip', 'slab')
The draws below stay inside these ranges and needn't reach their ends.
Inputs may be any that keep to these rules, and one draw needn't show every extreme that they name: `owner`: every index of trip owns exactly 4 occupied spinors. `triples`: the first index i is the same in every triple; in each slot m all groups share j; the k of group g is owned by index g of trip; i, j, k of a triple are distinct.
All inputs are finite; a program needn't handle non-finite values.
Results may differ from the reference program's by a relative error of at most 0.0001.
Values sent between devices are 32-bit elements; how exact they have to be, the bound alone decides.
No kernel may reach another device: no remote copies, remote signals or barrier semaphores. Data moves between devices by JAX's collectives and lax.ppermute only.
A program may use at most 192 MiB of HBM per device.

```python
import jax
import jax.numpy as jnp
from jax import lax

OCCUPIED_COUNT = 32
V = 256
TRIPLES_PER_GROUP = 2
OCCUPIED_LOCAL = 4
N_TRIP = 8


def occupied_order(key):
    return jax.random.permutation(jax.random.fold_in(key, 11), OCCUPIED_COUNT).astype(jnp.int32)


def draw_owner(key, part):
    order = occupied_order(key)
    return jnp.zeros((OCCUPIED_COUNT,), jnp.int32).at[order].set((jnp.arange(OCCUPIED_COUNT, dtype=jnp.int32) // OCCUPIED_LOCAL).astype(jnp.int32))


def draw_triples(key, part):
    order = occupied_order(key)
    key = jax.random.fold_in(key, 5)
    first_key, middle_random_key, trailing_random_key = jax.random.split(key, 3)
    occupied_i = jax.random.randint(first_key, (), 0, OCCUPIED_COUNT - 1).astype(jnp.int32)
    occupied_j = ((occupied_i + 1 + jax.random.randint(middle_random_key, (TRIPLES_PER_GROUP,), 0, OCCUPIED_COUNT - 1)) % OCCUPIED_COUNT).astype(jnp.int32)
    occupied_j = occupied_j.at[0].set(OCCUPIED_COUNT - 1).astype(jnp.int32)
    candidate_rows = order.reshape(N_TRIP, OCCUPIED_LOCAL)
    score_values = jax.random.randint(trailing_random_key, (TRIPLES_PER_GROUP, N_TRIP, OCCUPIED_LOCAL), 0, 1 << 20) * OCCUPIED_LOCAL + jnp.arange(OCCUPIED_LOCAL, dtype=jnp.int32)[None, None, :]
    taken = (candidate_rows[None, :, :] == occupied_i) | (candidate_rows[None, :, :] == occupied_j[:, None, None])
    score_values = score_values + taken.astype(jnp.int32) * (OCCUPIED_LOCAL << 21)
    chosen_index = jnp.argmin(score_values, axis=2).astype(jnp.int32)
    occupied_k = jnp.take_along_axis(jnp.broadcast_to(candidate_rows[None], (TRIPLES_PER_GROUP, N_TRIP, OCCUPIED_LOCAL)), chosen_index[:, :, None], axis=2)[:, :, 0]
    leading_index = jnp.broadcast_to(occupied_i, (TRIPLES_PER_GROUP, N_TRIP))
    middle_index = jnp.broadcast_to(occupied_j[:, None], (TRIPLES_PER_GROUP, N_TRIP))
    return jnp.stack([leading_index, middle_index, occupied_k], axis=-1).astype(jnp.int32)


def levels(rng, shape, shards, low, high):
    level, own = 1.0, jax.random.fold_in(rng, 6)
    for dim, parts in shards:
        steps = jnp.exp(jax.random.uniform(jax.random.fold_in(own, dim), (parts,), jnp.float32, low / len(shards), high / len(shards)))
        level = level * jnp.repeat(steps, shape[dim] // parts).reshape([-1 if axis == dim else 1 for axis in range(len(shape))])
    return level


def normal_values(rng, dims, width, reach, pieces=(), kind=jnp.bfloat16):
    result = jax.random.normal(rng, dims, jnp.float32) * width
    if len(pieces) > 0:
        result = levels(rng, dims, pieces, -0.22, 0.18) * result
    return jnp.clip(result, min=-reach, max=reach).astype(kind)


def setup_inputs(seed: int = 0) -> dict:
    key_of = jax.random.split(jax.random.key(seed), 7)
    integrals = normal_values(key_of[0], (OCCUPIED_COUNT, V, V, V), 0.04, 0.24, ((0, 8), (1, 16)), jnp.float32)
    amplitudes = normal_values(key_of[1], (OCCUPIED_COUNT, OCCUPIED_COUNT, V, V), 1.0, 6.0, ((0, 8), (1, 16)), jnp.float32)
    occ_energy = jnp.clip(jax.random.uniform(key_of[2], (OCCUPIED_COUNT,), jnp.float32, -3.0, -1.0), -3.0, -1.0)
    vir_energy = jnp.clip(jax.random.uniform(key_of[3], (V,), jnp.float32, 0.5, 3.0), 0.5, 3.0)
    owner = draw_owner(jax.random.fold_in(key_of[6], 71), 0)
    triples = draw_triples(jax.random.fold_in(key_of[6], 71), 0)
    return {"integrals": integrals, "amplitudes": amplitudes, "occ_energy": occ_energy, "vir_energy": vir_energy, "owner": owner, "triples": triples}


def ranks(owner):
    count = owner.shape[0]
    index = jnp.arange(count, dtype=jnp.int32)
    earlier = (owner[None, :] == owner[:, None]) & (index[None, :] < index[:, None])
    return jnp.sum(earlier.astype(jnp.int32), axis=1).astype(jnp.int32)


def reference(integrals, amplitudes, occ_energy, vir_energy, owner, triples):
    high = lax.Precision.HIGHEST
    storage = (owner * (OCCUPIED_COUNT // N_TRIP) + ranks(owner)).astype(jnp.int32)
    vir_sum = vir_energy[:, None, None] + vir_energy[None, :, None] + vir_energy[None, None, :]
    residual = jnp.zeros((OCCUPIED_COUNT, OCCUPIED_COUNT, V, V), jnp.float32)
    for triple_position in range(TRIPLES_PER_GROUP):
        for group in range(N_TRIP):
            occupied_i = triples[triple_position, group, 0]
            occupied_j = triples[triple_position, group, 1]
            occupied_k = triples[triple_position, group, 2]
            w_i = integrals[storage[occupied_i]]
            w_j = integrals[storage[occupied_j]]
            w_k = integrals[storage[occupied_k]]
            t_ij = amplitudes[storage[occupied_i], occupied_j]
            t_jk = amplitudes[storage[occupied_j], occupied_k]
            t_ki = amplitudes[storage[occupied_k], occupied_i]
            connected = jnp.einsum("ad,cdb->acb", t_ij, w_k, precision=high)
            connected = connected + jnp.einsum("ad,cdb->acb", t_jk, w_i, precision=high)
            connected = connected + jnp.einsum("ad,cdb->acb", t_ki, w_j, precision=high)
            shift = occ_energy[occupied_i] + occ_energy[occupied_j] + occ_energy[occupied_k]
            triple_amp = connected / (shift - vir_sum)
            r_ij = jnp.einsum("acb,cdb->ad", triple_amp, w_k, precision=high)
            r_jk = jnp.einsum("acb,cdb->ad", triple_amp, w_i, precision=high)
            r_ki = jnp.einsum("acb,cdb->ad", triple_amp, w_j, precision=high)
            residual = residual.at[storage[occupied_i], occupied_j].add(r_ij)
            residual = residual.at[storage[occupied_j], occupied_k].add(r_jk)
            residual = residual.at[storage[occupied_k], occupied_i].add(r_ki)
    return residual
```

```python
import jax
import jax.numpy as jnp
from jax import lax
from jax.experimental import pallas as pl
from jax.experimental.pallas import tpu as pltpu
from jax.sharding import PartitionSpec as P

GRAY = (0, 1, 3, 2)
CUBE = tuple((t // 4) * 4 + GRAY[t % 4] for t in range(8))
FROM_CUBE = tuple(CUBE.index(v) for v in range(8))
ALONG = tuple([(t, FROM_CUBE[CUBE[t] ^ (1 << d)]) for t in range(8)] for d in range(3))

ARRIVE = [[None] * 8 for _ in range(3)]
FORWARD = [[0] * 8 for _ in range(3)]
for p in range(3):
    q, r = (p + 1) % 3, (p + 2) % 3
    a, b, c = 1 << p, 1 << q, 1 << r
    for node, depth, dim in ((a, 1, p), (a | b, 2, q), (a | c, 2, r), (7, 3, r), (b, 3, p), (c, 3, p), (b | c, 4, p)):
        ARRIVE[p][node] = (depth, dim)
    for node, dim in ((a, q), (a, r), (a | b, r), (a | b, p), (a | c, p), (7, p)):
        FORWARD[dim][node] = 1 + ARRIVE[p][node][1]
KINDS = [sorted(set(ARRIVE[p][1:])) for p in range(3)]
ARRIVAL = [[0] + [1 + KINDS[p].index(kind) for kind in ARRIVE[p][1:]] for p in range(3)]

ROWS = 2
PLACE, PLACE_K, SOURCE, ARRIVED, OWNER, OCC, OCC_K, ALL_K, TRIP, SLAB, TABLE = 0, 3, 5, 14, 23, 26, 29, 31, 47, 48, 49

HBM = pl.BlockSpec(memory_space=pltpu.HBM)
SMEM = pl.BlockSpec(memory_space=pltpu.SMEM)
VMEM = pl.BlockSpec(memory_space=pltpu.VMEM)


def pick(values, index):
    found = jnp.int32(values[0])
    for n in range(1, len(values)):
        found = jnp.where(index == n, jnp.int32(values[n]), found)
    return found


def call(kernel, out_shape, operands, specs, out_specs=None, scratch=(), mib=49, cost=(0, 1 << 20), aliases=None):
    return pl.pallas_call(
        kernel,
        in_specs=list(specs),
        out_specs=out_specs,
        out_shape=out_shape,
        scratch_shapes=list(scratch),
        input_output_aliases=aliases or {},
        cost_estimate=pl.CostEstimate(flops=cost[0], bytes_accessed=cost[1], transcendentals=0),
        compiler_params=pltpu.CompilerParams(vmem_limit_bytes=mib * 2**20),
    )(*operands)


def f32(*shape):
    return jax.ShapeDtypeStruct(shape, jnp.float32)


def table_kernel(owner_ref, triples_ref, where_ref, out_ref):
    count = owner_ref.shape[0]
    trip = where_ref[0]
    out_ref[TRIP], out_ref[SLAB] = trip, where_ref[1]
    groups = triples_ref.shape[0] // 6

    def triple(m, g, n):
        return triples_ref[(m * groups + g) * 3 + n]

    def rank(occ):
        mine = owner_ref[occ]
        total = jnp.int32(0)
        for other in range(count):
            total += ((other < occ) & (owner_ref[other] == mine)).astype(jnp.int32)
        return total

    for x, occ in enumerate((triple(0, 0, 0), triple(0, 0, 1), triple(1, 0, 1))):
        owner = owner_ref[occ]
        rho = pick(CUBE, trip) ^ pick(CUBE, owner)
        out_ref[PLACE + x], out_ref[OWNER + x], out_ref[OCC + x] = rank(occ), owner, occ
        for n in range(3):
            out_ref[SOURCE + 3 * x + n] = pick(FORWARD[n], rho)
            out_ref[ARRIVED + 3 * x + n] = pick(ARRIVAL[n], rho)
    for m in range(2):
        occ = triple(m, trip, 2)
        out_ref[PLACE_K + m], out_ref[OCC_K + m] = rank(occ), occ
        for g in range(groups):
            out_ref[ALL_K + m * groups + g] = triple(m, g, 2)


def run(copies):
    for copy in copies:
        copy.start()
    for copy in copies:
        copy.wait()


def thirds(size):
    height = -(-size // 24) * 8
    return height, (0, height, size - height)


def own_part(integrals_ref, table_ref, x, chunk, p, low=0):
    height, offsets = thirds(integrals_ref.shape[2])
    return integrals_ref.at[
        table_ref[PLACE + x], pl.ds(chunk * ROWS, ROWS), pl.ds(offsets[p] + low, height - low), :
    ]


def send_kernel(chunk, table_ref, integrals_ref, *refs):
    got, sent, sems = refs[:-4], refs[-4:-1], refs[-1]
    copies = []
    for d in range(3):
        for x in range(3):
            source = table_ref[SOURCE + 3 * x + d] if got else jnp.int32(0)
            mine = pltpu.make_async_copy(
                own_part(integrals_ref, table_ref, x, chunk, d), sent[d].at[x], sems.at[3 * d + x]
            )
            pl.when(source == 0)(mine.start)
            copies.append((source, mine))
    for d in range(3):
        for x in range(3):
            for e in range(len(got)):

                @pl.when(copies[3 * d + x][0] == 1 + e)
                def _():
                    sent[d][x] = got[e][x]

    for source, mine in copies:
        pl.when(source == 0)(mine.wait)


def send(chunk, table, integrals, got):
    size = integrals.shape[-1]
    height, _ = thirds(size)
    shape = f32(3, ROWS, height, size)
    return call(
        lambda *refs: send_kernel(chunk, *refs),
        (shape,) * 3,
        (table, integrals, *got),
        (SMEM, HBM) + (VMEM,) * len(got),
        (VMEM,) * 3,
        (pltpu.SemaphoreType.DMA((9,)),),
        cost=(0, 6 * 4 * shape.size),
    )


def split(value):
    high = value.astype(jnp.bfloat16)
    return high, (value - high.astype(jnp.float32)).astype(jnp.bfloat16)


def product(left, right, dims):
    total = None
    for x, y in ((left[0], right[0]), (left[0], right[1]), (left[1], right[0])):
        term = lax.dot_general(x, y, (dims, ((), ())), preferred_element_type=jnp.float32)
        total = term if total is None else total + term
    return total


def rows_kernel(chunk, first, last, table_ref, occ_ref, vir_c_ref, vir_a_ref, vir_b_ref, t_ref, integrals_ref, *refs):
    got, rest = refs[:12], refs[12:]
    if not first:
        in_ref, rest = rest[0], rest[1:]
    if last:
        keep_ref, give_ref, w_ref, k_ref, high_ref, low_ref, sems, out_ref = rest
    else:
        out_ref, w_ref, k_ref, high_ref, low_ref, sems = rest
    size = w_ref.shape[-1]
    height, offsets = thirds(size)

    copies = []
    for m in range(2):
        mine = pltpu.make_async_copy(
            integrals_ref.at[table_ref[PLACE_K + m], pl.ds(chunk * ROWS, ROWS)], k_ref.at[m], sems.at[9 + m]
        )
        mine.start()
        copies.append(mine)
    for x in range(3):
        for p in range(3):
            low = offsets[1] + height - offsets[2] if p == 2 else 0
            target = w_ref.at[x, :, pl.ds(offsets[p] + low, height - low), :]
            sem = sems.at[3 * x + p]
            arrived = table_ref[ARRIVED + 3 * x + p]
            mine = pltpu.make_async_copy(own_part(integrals_ref, table_ref, x, chunk, p, low), target, sem)
            pl.when(arrived == 0)(mine.start)
            for kind, (depth, dim) in enumerate(KINDS[p]):
                source = got[3 * (depth - 1) + dim].at[x, :, pl.ds(low, height - low), :]
                pl.when(arrived == 1 + kind)(pltpu.make_async_copy(source, target, sem).start)
            copies.append(mine)
    for m in range(2):
        high, low = split(t_ref[:, m].reshape(size, 3 * size))
        high_ref[m], low_ref[m] = high, low
    out_ref[...] = jnp.zeros_like(out_ref) if first else in_ref[...]
    virs = vir_a_ref[...] + vir_b_ref[...]
    shift_ij = [occ_ref[table_ref[OCC]] + occ_ref[table_ref[OCC + 1 + m]] for m in range(2)]
    shifts = [shift_ij[m] + occ_ref[table_ref[OCC_K + m]] for m in range(2)]
    for copy in copies:
        copy.wait()

    @pl.loop(0, ROWS)
    def _(row):
        c = table_ref[SLAB] * integrals_ref.shape[1] + chunk * ROWS + row
        shared = [split(w_ref[x, row]) for x in range(3)]
        for m in range(2):
            blocks = (split(k_ref[m, row]), shared[0], shared[1 + m])
            connected = None
            for b, block in enumerate(blocks):
                columns = slice(b * size, (b + 1) * size)
                term = product((high_ref[m, :, columns], low_ref[m, :, columns]), block, ((1,), (0,)))
                connected = term if connected is None else connected + term
            amp = split(connected / (shifts[m] - (virs + vir_c_ref[c])))
            for b, block in enumerate(blocks):
                term = product(amp, block, ((1,), (1,)))
                columns = slice(b * size, (b + 1) * size)
                out_ref[:, m, :, columns] += term.reshape(out_ref.shape[0], -1, size)

    if last:
        core = lax.rem(table_ref[SLAB], 2)
        for chip in range(keep_ref.shape[0]):
            keep_ref[chip] = out_ref[2 * chip + core]
            give_ref[chip] = out_ref[2 * chip + 1 - core]


def rows(chunk, last, table, occ, vir, t, integrals, got, total):
    size = integrals.shape[-1]
    used = [buffer for step in got[chunk : chunk + 4] for buffer in step]
    first = total is None
    operands = (table, occ, vir, vir[:, None], vir[None, :], t, integrals, *used) + (() if first else (total,))
    specs = (SMEM, SMEM, SMEM, VMEM, VMEM, VMEM) + (HBM,) * 13 + (() if first else (VMEM,))
    half = f32(t.shape[0] // 2, *t.shape[1:])
    scratch = (
        pltpu.VMEM((3, ROWS, size, size), jnp.float32),
        pltpu.VMEM((2, ROWS, size, size), jnp.float32),
        pltpu.VMEM((2, size, 3 * size), jnp.bfloat16),
        pltpu.VMEM((2, size, 3 * size), jnp.bfloat16),
        pltpu.SemaphoreType.DMA((11,)),
    )
    return call(
        lambda *refs: rows_kernel(chunk, first, last, *refs),
        (half, half) if last else f32(*t.shape),
        operands,
        specs,
        (VMEM, VMEM) if last else VMEM,
        scratch + ((pltpu.VMEM(t.shape, jnp.float32),) if last else ()),
        cost=(ROWS * 36 * 2 * size**3, ROWS * 20 * size**2 + 12 * t.size),
    )


def to_slabs_kernel(table_ref, amplitudes_ref, out_ref, sems):
    q_slab = amplitudes_ref.shape[1]
    slots = [(PLACE + 1 + m, q) for m in range(2) for q in range(q_slab)]
    slots += [(PLACE_K + m, lax.rem(table_ref[OCC], q_slab)) for m in range(2)]
    slots += [(PLACE, lax.rem(table_ref[OCC + 1 + m], q_slab)) for m in range(2)]
    run(
        [
            pltpu.make_async_copy(amplitudes_ref.at[table_ref[row], q], out_ref.at[:, n], sems.at[n])
            for n, (row, q) in enumerate(slots)
        ]
    )


def to_groups_kernel(q_slab, table_ref, by_slab_ref, out_ref):
    groups = out_ref.shape[0]
    for m in range(2):
        j = table_ref[OCC + 1 + m]
        value = by_slab_ref[lax.div(j, q_slab), 2 * q_slab + 2 + m]
        for g in range(groups):
            k = table_ref[ALL_K + m * groups + g]
            out_ref[g, m] = by_slab_ref[lax.div(k, q_slab), q_slab * m + lax.rem(k, q_slab)]
            out_ref[g, 2 + m] = value


def my_pairs_kernel(q_slab, table_ref, by_slab_ref, by_trip_ref, out_ref):
    size = by_slab_ref.shape[-1]
    for m in range(2):
        pairs = (
            by_trip_ref[table_ref[OWNER], 2 + m],
            by_trip_ref[table_ref[OWNER + 1 + m], m],
            by_slab_ref[lax.div(table_ref[OCC], q_slab), 2 * q_slab + m],
        )
        for slab in range(out_ref.shape[0]):
            for n, value in enumerate(pairs):
                out_ref[slab, m, :, n * size : (n + 1) * size] = value


def sums_kernel(in_ref, ki_ref, out_ref):
    size = ki_ref.shape[-1]
    sums = jnp.sum(in_ref[...], axis=0)
    ki_ref[...] = sums[:, :, 2 * size :]
    for g in range(out_ref.shape[0]):
        out_ref[g, :2] = sums[:, :, size : 2 * size]
        out_ref[g, 2:] = sums[:, :, :size]


def place_kernel(rows_count, q_slab, table_ref, ki_ref, arrived_ref, out_ref):
    groups = arrived_ref.shape[0]
    out_ref[...] = jnp.zeros_like(out_ref)

    def cell(col, row):
        return (lax.div(col, q_slab) * rows_count + row) * q_slab + lax.rem(col, q_slab)

    for m in range(2):
        out_ref[cell(table_ref[OCC], table_ref[PLACE_K + m])] += ki_ref[m]

        @pl.when(table_ref[OWNER] == table_ref[TRIP])
        def _():
            out_ref[cell(table_ref[OCC + 1 + m], table_ref[PLACE])] += jnp.sum(arrived_ref[:, 2 + m], axis=0)

        @pl.when(table_ref[OWNER + 1 + m] == table_ref[TRIP])
        def _():
            for g in range(groups):
                out_ref[cell(table_ref[ALL_K + m * groups + g], table_ref[PLACE + 1 + m])] += arrived_ref[g, m]


def on_device(integrals, amplitudes, occ_energy, vir_energy, owner, triples):
    n_slab, n_trip = lax.axis_size("slab"), lax.axis_size("trip")
    rows_count, q_slab, size = amplitudes.shape[:3]
    part = size // n_slab
    where = jnp.stack([lax.axis_index("trip"), lax.axis_index("slab")]).astype(jnp.int32)
    table = call(
        table_kernel,
        jax.ShapeDtypeStruct((TABLE,), jnp.int32),
        (owner, triples.reshape(-1), where),
        (SMEM,) * 3,
        SMEM,
        cost=(0, 1 << 10),
    )

    slots = 2 * q_slab + 4
    to_slabs = call(
        to_slabs_kernel,
        f32(n_slab, slots, part, size),
        (table, amplitudes.reshape(rows_count, q_slab, n_slab, part, size)),
        (SMEM, HBM),
        VMEM,
        (pltpu.SemaphoreType.DMA((slots,)),),
        cost=(0, 8 * slots * size**2),
    )
    table, to_slabs = lax.optimization_barrier((table, to_slabs))
    by_slab = lax.all_to_all(to_slabs, "slab", 0, 0, tiled=True)
    to_groups = call(
        lambda *refs: to_groups_kernel(q_slab, *refs),
        f32(n_trip, 4, part, size),
        (table, by_slab),
        (SMEM, VMEM),
        VMEM,
        cost=(0, 32 * n_trip * part * size),
    )

    chunks = integrals.shape[1] // ROWS
    got, total, t = [], None, None
    ready = 0
    for step in range(chunks + 3):
        previous = tuple(got[-1]) if got else ()
        if step == 2:
            to_groups, *previous = lax.optimization_barrier((to_groups, *previous))
            by_trip = lax.all_to_all(to_groups, "trip", 0, 0, tiled=True)
            pairs = call(
                lambda *refs: my_pairs_kernel(q_slab, *refs),
                f32(n_slab, 2, part, 3 * size),
                (table, by_slab, by_trip),
                (SMEM, VMEM, VMEM),
                VMEM,
                cost=(0, 8 * 6 * size**2),
            )
        if step == 4:
            pairs, *previous = lax.optimization_barrier((pairs, *previous))
            t = lax.all_to_all(pairs, "slab", 0, 0, tiled=True)
        if total is not None:
            total, *previous = lax.optimization_barrier((total, *previous))
        sent = send(min(step, chunks - 1), table, integrals, previous)
        got.append([lax.ppermute(sent[d], "trip", ALONG[d]) for d in range(3)])
        while t is not None and step > 4 and ready + 3 < (len(got) if step == chunks + 2 else step):
            total = rows(ready, ready == chunks - 1, table, occ_energy, vir_energy, t, integrals, got, total)
            ready += 1

    keep, give = total
    give = lax.ppermute(give, "slab", [(slab, slab ^ 1) for slab in range(n_slab)])
    same_core = [list(range(core, n_slab, 2)) for core in range(2)]
    by_slab = lax.all_to_all(keep + give, "slab", 0, 0, axis_index_groups=same_core, tiled=True)
    r_ki, outgoing = call(
        sums_kernel,
        (f32(2, part, size), f32(n_trip, 4, part, size)),
        (by_slab,),
        (VMEM,),
        (VMEM, VMEM),
    )
    arrived = lax.all_to_all(outgoing, "trip", 0, 0, tiled=True)
    spread = call(
        lambda *refs: place_kernel(rows_count, q_slab, *refs),
        f32(n_slab * rows_count * q_slab, part, size),
        (table, r_ki, arrived),
        (SMEM, VMEM, VMEM),
        VMEM,
    )
    result = lax.all_to_all(spread.reshape(n_slab, -1, part, size), "slab", 0, 0, tiled=True)
    return jnp.swapaxes(result, 0, 1).reshape(amplitudes.shape)


def solution(mesh):
    in_specs = (P("trip", "slab", None, None), P("trip", "slab", None, None), P(), P(), P(), P())
    out_specs = P("trip", "slab", None, None)
    return jax.shard_map(
        on_device, mesh=mesh, in_specs=in_specs, out_specs=out_specs, check_vma=False
    )
```

```python
import jax
import jax.numpy as jnp
from jax import lax
from jax.experimental import pallas as pl
from jax.experimental.pallas import tpu as pltpu
from jax.sharding import PartitionSpec as P

GRAY = (0, 1, 3, 2)
CUBE = tuple((t // 4) * 4 + GRAY[t % 4] for t in range(8))
FROM_CUBE = tuple(CUBE.index(v) for v in range(8))
ALONG = tuple([(t, FROM_CUBE[CUBE[t] ^ (1 << d)]) for t in range(8)] for d in range(3))

ARRIVE = [[None] * 8 for _ in range(3)]
FORWARD = [[0] * 8 for _ in range(3)]
for p in range(3):
    q, r = (p + 1) % 3, (p + 2) % 3
    a, b, c = 1 << p, 1 << q, 1 << r
    for node, depth, dim in ((a, 1, p), (a | b, 2, q), (a | c, 2, r), (7, 3, r), (b, 3, p), (c, 3, p), (b | c, 4, p)):
        ARRIVE[p][node] = (depth, dim)
    for node, dim in ((a, q), (a, r), (a | b, r), (a | b, p), (a | c, p), (7, p)):
        FORWARD[dim][node] = 1 + ARRIVE[p][node][1]
KINDS = [sorted(set(ARRIVE[p][1:])) for p in range(3)]
ARRIVAL = [[0] + [1 + KINDS[p].index(kind) for kind in ARRIVE[p][1:]] for p in range(3)]

PARTS = 8
ROWS = 2
PLACE, PLACE_K, SOURCE, ARRIVED, OWNER, OCC, OCC_K, ALL_K, TRIP, SLAB, TABLE = 0, 3, 5, 14, 23, 26, 29, 31, 47, 48, 49

HBM = pl.BlockSpec(memory_space=pltpu.HBM)
SMEM = pl.BlockSpec(memory_space=pltpu.SMEM)
VMEM = pl.BlockSpec(memory_space=pltpu.VMEM)


def pick(values, index):
    found = jnp.int32(values[0])
    for n in range(1, len(values)):
        found = jnp.where(index == n, jnp.int32(values[n]), found)
    return found


def call(kernel, out_shape, operands, specs, out_specs=None, scratch=(), mib=49, cost=(0, 1 << 20), aliases=None):
    return pl.pallas_call(
        kernel,
        in_specs=list(specs),
        out_specs=out_specs,
        out_shape=out_shape,
        scratch_shapes=list(scratch),
        input_output_aliases=aliases or {},
        cost_estimate=pl.CostEstimate(flops=cost[0], bytes_accessed=cost[1], transcendentals=0),
        compiler_params=pltpu.CompilerParams(vmem_limit_bytes=mib * 2**20),
    )(*operands)


def f32(*shape):
    return jax.ShapeDtypeStruct(shape, jnp.float32)


def table_kernel(owner_ref, triples_ref, where_ref, out_ref):
    count = owner_ref.shape[0]
    trip = where_ref[0]
    out_ref[TRIP], out_ref[SLAB] = trip, where_ref[1]
    groups = triples_ref.shape[0] // 6

    def triple(m, g, n):
        return triples_ref[(m * groups + g) * 3 + n]

    def rank(occ):
        mine = owner_ref[occ]
        total = jnp.int32(0)
        for other in range(count):
            total += ((other < occ) & (owner_ref[other] == mine)).astype(jnp.int32)
        return total

    for x, occ in enumerate((triple(0, 0, 0), triple(0, 0, 1), triple(1, 0, 1))):
        owner = owner_ref[occ]
        rho = pick(CUBE, trip) ^ pick(CUBE, owner)
        out_ref[PLACE + x], out_ref[OWNER + x], out_ref[OCC + x] = rank(occ), owner, occ
        for n in range(3):
            out_ref[SOURCE + 3 * x + n] = pick(FORWARD[n], rho)
            out_ref[ARRIVED + 3 * x + n] = pick(ARRIVAL[n], rho)
    for m in range(2):
        occ = triple(m, trip, 2)
        out_ref[PLACE_K + m], out_ref[OCC_K + m] = rank(occ), occ
        for g in range(groups):
            out_ref[ALL_K + m * groups + g] = triple(m, g, 2)


def pairs_of(table_ref, groups, q_slab):
    found = [(m, PLACE_K + m, OCC, None) for m in range(2)]
    found += [(m, PLACE, OCC + 1 + m, OWNER) for m in range(2)]
    found += [(m, PLACE + 1 + m, ALL_K + m * groups + g, OWNER + 1 + m) for m in range(2) for g in range(groups)]
    pairs = []
    for m, row, col, plane in found:
        slab, q = lax.div(table_ref[col], q_slab), lax.rem(table_ref[col], q_slab)
        here = True if plane is None else table_ref[plane] == table_ref[TRIP]
        pairs.append((table_ref[row], slab, q, m * q_slab + q, here))
    return pairs


def thirds(size):
    height = -(-size // 24) * 8
    return height, (0, height, size - height)


def own_part(integrals_ref, table_ref, x, chunk, p, low=0):
    height, offsets = thirds(integrals_ref.shape[2])
    return integrals_ref.at[
        table_ref[PLACE + x], pl.ds(chunk * ROWS, ROWS), pl.ds(offsets[p] + low, height - low), :
    ]


def send_kernel(chunk, table_ref, integrals_ref, *refs):
    got, sent, sems = refs[:-4], refs[-4:-1], refs[-1]
    copies = []
    for d in range(3):
        for x in range(3):
            source = table_ref[SOURCE + 3 * x + d] if got else jnp.int32(0)
            mine = pltpu.make_async_copy(
                own_part(integrals_ref, table_ref, x, chunk, d), sent[d].at[x], sems.at[3 * d + x]
            )
            pl.when(source == 0)(mine.start)
            copies.append((source, mine))
    for d in range(3):
        for x in range(3):
            for e in range(len(got)):

                @pl.when(copies[3 * d + x][0] == 1 + e)
                def _():
                    sent[d][x] = got[e][x]

    for source, mine in copies:
        pl.when(source == 0)(mine.wait)


def send(chunk, table, integrals, got):
    size = integrals.shape[-1]
    height, _ = thirds(size)
    shape = f32(3, ROWS, height, size)
    return call(
        lambda *refs: send_kernel(chunk, *refs),
        (shape,) * 3,
        (table, integrals, *got),
        (SMEM, HBM) + (VMEM,) * len(got),
        (VMEM,) * 3,
        (pltpu.SemaphoreType.DMA((9,)),),
        cost=(0, 6 * 4 * shape.size),
    )


def split(value):
    high = value.astype(jnp.bfloat16)
    return high, (value - high.astype(jnp.float32)).astype(jnp.bfloat16)


def product(highs, lows, block, dims):
    size, count = highs[0].shape[0], len(highs)

    def dot(parts, right):
        left = parts[0] if len(parts) == 1 else jnp.concatenate(parts)
        return lax.dot_general(left, right, (dims, ((), ())), preferred_element_type=jnp.float32)

    both, rest = dot(highs + lows, block[0]), dot(highs, block[1])
    part = lambda value, n: value[n * size : (n + 1) * size]
    return [part(both, n) + part(both, count + n) + part(rest, n) for n in range(count)]


def rows_kernel(chunk, first, last, table_ref, occ_ref, vir_c_ref, vir_a_ref, vir_b_ref, high_ref, low_ref, integrals_ref, *refs):
    got, rest = refs[:12], refs[12:]
    if not first:
        in_ref, rest = rest[0], rest[1:]
    if last:
        keep_ref, give_ref, w_ref, k_ref, sems, out_ref = rest
    else:
        out_ref, w_ref, k_ref, sems = rest
    size = w_ref.shape[-1]
    height, offsets = thirds(size)

    copies = []
    for m in range(2):
        mine = pltpu.make_async_copy(
            integrals_ref.at[table_ref[PLACE_K + m], pl.ds(chunk * ROWS, ROWS)], k_ref.at[m], sems.at[9 + m]
        )
        mine.start()
        copies.append(mine)
    for x in range(3):
        for p in range(3):
            low = offsets[1] + height - offsets[2] if p == 2 else 0
            target = w_ref.at[x, :, pl.ds(offsets[p] + low, height - low), :]
            sem = sems.at[3 * x + p]
            arrived = table_ref[ARRIVED + 3 * x + p]
            mine = pltpu.make_async_copy(own_part(integrals_ref, table_ref, x, chunk, p, low), target, sem)
            pl.when(arrived == 0)(mine.start)
            for kind, (depth, dim) in enumerate(KINDS[p]):
                source = got[3 * (depth - 1) + dim].at[x, :, pl.ds(low, height - low), :]
                pl.when(arrived == 1 + kind)(pltpu.make_async_copy(source, target, sem).start)
            copies.append(mine)
    out_ref[...] = jnp.zeros_like(out_ref) if first else in_ref[...]
    virs = vir_a_ref[...] + vir_b_ref[...]
    shift_ij = [occ_ref[table_ref[OCC]] + occ_ref[table_ref[OCC + 1 + m]] for m in range(2)]
    shifts = [shift_ij[m] + occ_ref[table_ref[OCC_K + m]] for m in range(2)]
    for copy in copies:
        copy.wait()

    @pl.loop(0, ROWS)
    def _(row):
        c = table_ref[SLAB] * integrals_ref.shape[1] + chunk * ROWS + row
        shared = [split(w_ref[x, row]) for x in range(3)]
        blocks = [[split(k_ref[m, row]) for m in range(2)], [shared[0]], [shared[1], shared[2]]]

        def against(highs, lows, dims):
            found = []
            for b in range(3):
                if len(blocks[b]) == 1:
                    found.append(product([highs(m, b) for m in range(2)], [lows(m, b) for m in range(2)], blocks[b][0], dims))
                else:
                    found.append([product([highs(m, b)], [lows(m, b)], blocks[b][m], dims)[0] for m in range(2)])
            return found

        terms = against(lambda m, b: high_ref[m, b], lambda m, b: low_ref[m, b], ((1,), (0,)))
        amps = []
        for m in range(2):
            connected = terms[0][m] + terms[1][m] + terms[2][m]
            amps.append(split(connected / (shifts[m] - (virs + vir_c_ref[c]))))
        terms = against(lambda m, b: amps[m][0], lambda m, b: amps[m][1], ((1,), (1,)))
        for m in range(2):
            for b in range(3):
                out_ref[:, m, :, b * size : (b + 1) * size] += terms[b][m].reshape(out_ref.shape[0], -1, size)

    if last:
        core = lax.rem(table_ref[SLAB], 2)
        for chip in range(keep_ref.shape[0]):
            keep_ref[chip] = out_ref[2 * chip + core]
            give_ref[chip] = out_ref[2 * chip + 1 - core]


def rows(chunk, last, table, occ, vir, highs, lows, integrals, got, total):
    size = integrals.shape[-1]
    used = [buffer for step in got[chunk : chunk + 4] for buffer in step]
    first = total is None
    operands = (table, occ, vir, vir[:, None], vir[None, :], highs, lows, integrals, *used) + (() if first else (total,))
    specs = (SMEM, SMEM, SMEM, VMEM, VMEM, VMEM, VMEM) + (HBM,) * 13 + (() if first else (VMEM,))
    shape = (2 * PARTS, 2, size // (2 * PARTS), 3 * size)
    half = f32(PARTS, *shape[1:])
    scratch = (
        pltpu.VMEM((3, ROWS, size, size), jnp.float32),
        pltpu.VMEM((2, ROWS, size, size), jnp.float32),
        pltpu.SemaphoreType.DMA((11,)),
    )
    return call(
        lambda *refs: rows_kernel(chunk, first, last, *refs),
        (half, half) if last else f32(*shape),
        operands,
        specs,
        (VMEM, VMEM) if last else VMEM,
        scratch + ((pltpu.VMEM(shape, jnp.float32),) if last else ()),
        cost=(ROWS * 36 * 2 * size**3, ROWS * 20 * size**2 + 12 * 6 * size**2),
    )


def to_slabs_kernel(table_ref, amplitudes_ref, out_ref, sems):
    copies = []
    for n, (row, slab, q, slot, here) in enumerate(pairs_of(table_ref, (sems.shape[0] - 4) // 2, amplitudes_ref.shape[1])):
        copy = pltpu.make_async_copy(amplitudes_ref.at[row, q], out_ref.at[:, slot], sems.at[n])
        mine = here & (slab == table_ref[SLAB])
        pl.when(mine)(copy.start)
        copies.append((mine, copy))
    for mine, copy in copies:
        pl.when(mine)(copy.wait)


def to_groups_kernel(q_slab, table_ref, by_slab_ref, ki_ref, out_ref):
    groups = out_ref.shape[0]
    parts = [(slab, slot) for _, slab, _, slot, _ in pairs_of(table_ref, groups, q_slab)]
    for m in range(2):
        ki_ref[m] = by_slab_ref[parts[m]]
        value = by_slab_ref[parts[2 + m]]
        for g in range(groups):
            out_ref[g, m] = by_slab_ref[parts[4 + m * groups + g]]
            out_ref[g, 2 + m] = value


def my_pairs_kernel(table_ref, ki_ref, by_trip_ref, out_ref):
    size = ki_ref.shape[-1]
    for m in range(2):
        pairs = (by_trip_ref[table_ref[OWNER], 2 + m], by_trip_ref[table_ref[OWNER + 1 + m], m], ki_ref[m])
        for chip in range(out_ref.shape[0]):
            for n, value in enumerate(pairs):
                out_ref[chip, m, :, n * size : (n + 1) * size] = value


def split_kernel(table_ref, mine_ref, other_ref, high_ref, low_ref):
    size = high_ref.shape[-1]
    core = lax.rem(table_ref[SLAB], 2)
    half = mine_ref.shape[2]
    for m in range(2):
        for n in range(3):
            for chip in range(mine_ref.shape[0]):
                for ref, parity in ((mine_ref, core), (other_ref, 1 - core)):
                    start = pl.multiple_of((2 * chip + parity) * half, half)
                    high, low = split(ref[chip, m, :, n * size : (n + 1) * size])
                    high_ref[m, n, pl.ds(start, half)] = high
                    low_ref[m, n, pl.ds(start, half)] = low


def sums_kernel(in_ref, ki_ref, out_ref):
    size = ki_ref.shape[-1]
    sums = jnp.sum(in_ref[...], axis=0)
    ki_ref[...] = sums[:, :, 2 * size :]
    for g in range(out_ref.shape[0]):
        out_ref[g, :2] = sums[:, :, size : 2 * size]
        out_ref[g, 2:] = sums[:, :, :size]


def from_groups_kernel(q_slab, table_ref, ki_ref, arrived_ref, out_ref):
    groups = arrived_ref.shape[0]
    for n, (_, slab, _, slot, here) in enumerate(pairs_of(table_ref, groups, q_slab)):

        @pl.when(here)
        def _():
            if n < 2:
                value = ki_ref[n]
            elif n < 4:
                value = jnp.sum(arrived_ref[:, n], axis=0)
            else:
                m, g = divmod(n - 4, groups)
                value = arrived_ref[g, m]
            out_ref[slab, slot] = value


def result_kernel(groups, table_ref, in_ref, out_ref):
    out_ref[...] = jnp.zeros_like(out_ref)
    for row, slab, q, slot, here in pairs_of(table_ref, groups, out_ref.shape[1]):

        @pl.when(here & (slab == table_ref[SLAB]))
        def _():
            out_ref[row, q] += in_ref[:, slot]


def on_device(integrals, amplitudes, occ_energy, vir_energy, owner, triples):
    n_slab, n_trip = lax.axis_size("slab"), lax.axis_size("trip")
    rows_count, q_slab, size = amplitudes.shape[:3]
    part = size // n_slab
    same_core = [list(range(core, n_slab, 2)) for core in range(2)]
    other_core = [(slab, slab ^ 1) for slab in range(n_slab)]
    where = jnp.stack([lax.axis_index("trip"), lax.axis_index("slab")]).astype(jnp.int32)
    table = call(
        table_kernel,
        jax.ShapeDtypeStruct((TABLE,), jnp.int32),
        (owner, triples.reshape(-1), where),
        (SMEM,) * 3,
        SMEM,
        cost=(0, 1 << 10),
    )
    amplitudes = amplitudes.reshape(rows_count, q_slab, n_slab, part, size)
    slots = 2 * q_slab

    chunks = integrals.shape[1] // ROWS
    got, total, pairs, parts = [], None, None, None
    ready = 0
    for step in range(chunks + 3):
        previous = tuple(got[-1]) if got else ()
        if step == 1:
            to_slabs = call(
                to_slabs_kernel,
                f32(n_slab, slots, part, size),
                (table, amplitudes),
                (SMEM, HBM),
                VMEM,
                (pltpu.SemaphoreType.DMA((4 + 2 * n_trip,)),),
                cost=(0, 8 * slots * size**2),
            )
            by_slab = lax.all_to_all(to_slabs, "slab", 0, 0, tiled=True)
            t_ki, to_groups = call(
                lambda *refs: to_groups_kernel(q_slab, *refs),
                (f32(2, part, size), f32(n_trip, 4, part, size)),
                (table, by_slab),
                (SMEM, VMEM),
                (VMEM, VMEM),
                cost=(0, 32 * n_trip * part * size),
            )
            t_ki, to_groups, *previous = lax.optimization_barrier((t_ki, to_groups, *previous))
        if step == 2:
            by_trip = lax.all_to_all(to_groups, "trip", 0, 0, tiled=True)
            pairs = call(
                my_pairs_kernel,
                f32(PARTS, 2, part, 3 * size),
                (table, t_ki, by_trip),
                (SMEM, VMEM, VMEM),
                VMEM,
                cost=(0, 4 * 6 * size**2),
            )
            pairs, *previous = lax.optimization_barrier((pairs, *previous))
        if step == 3:
            mine = lax.all_to_all(pairs, "slab", 0, 0, axis_index_groups=same_core, tiled=True)
            other = lax.ppermute(mine, "slab", other_core)
            shape = jax.ShapeDtypeStruct((2, 3, size, size), jnp.bfloat16)
            parts = call(
                split_kernel,
                (shape, shape),
                (table, mine, other),
                (SMEM, VMEM, VMEM),
                (VMEM, VMEM),
                cost=(0, 16 * 6 * size**2),
            )
        if total is not None:
            total, *previous = lax.optimization_barrier((total, *previous))
        sent = send(min(step, chunks - 1), table, integrals, previous)
        got.append([lax.ppermute(sent[d], "trip", ALONG[d]) for d in range(3)])
        while step > 3 and ready + 3 < (len(got) if step == chunks + 2 else step):
            total = rows(ready, ready == chunks - 1, table, occ_energy, vir_energy, *parts, integrals, got, total)
            ready += 1

    keep, give = total
    give = lax.ppermute(give, "slab", other_core)
    by_slab = lax.all_to_all(keep + give, "slab", 0, 0, axis_index_groups=same_core, tiled=True)
    r_ki, outgoing = call(
        sums_kernel,
        (f32(2, part, size), f32(n_trip, 4, part, size)),
        (by_slab,),
        (VMEM,),
        (VMEM, VMEM),
    )
    arrived = lax.all_to_all(outgoing, "trip", 0, 0, tiled=True)
    to_slabs = call(
        lambda *refs: from_groups_kernel(q_slab, *refs),
        f32(n_slab, slots, part, size),
        (table, r_ki, arrived),
        (SMEM, VMEM, VMEM),
        VMEM,
    )
    result = call(
        lambda *refs: result_kernel(n_trip, *refs),
        f32(*amplitudes.shape),
        (table, lax.all_to_all(to_slabs, "slab", 0, 0, tiled=True)),
        (SMEM, VMEM),
        VMEM,
    )
    return result.reshape(rows_count, q_slab, size, size)


def solution(mesh):
    in_specs = (P("trip", "slab", None, None), P("trip", "slab", None, None), P(), P(), P(), P())
    out_specs = P("trip", "slab", None, None)
    return jax.shard_map(
        on_device, mesh=mesh, in_specs=in_specs, out_specs=out_specs, check_vma=False
    )
```

```python
import jax
import jax.numpy as jnp
from jax import lax
from jax.experimental import pallas as pl
from jax.experimental.pallas import tpu as pltpu
from jax.sharding import PartitionSpec as P

GRAY = (0, 1, 3, 2)
CUBE = tuple((t // 4) * 4 + GRAY[t % 4] for t in range(8))
FROM_CUBE = tuple(CUBE.index(v) for v in range(8))
ALONG = tuple([(t, FROM_CUBE[CUBE[t] ^ (1 << d)]) for t in range(8)] for d in range(3))

ARRIVE = [[None] * 8 for _ in range(3)]
FORWARD = [[0] * 8 for _ in range(3)]
for p in range(3):
    q, r = (p + 1) % 3, (p + 2) % 3
    a, b, c = 1 << p, 1 << q, 1 << r
    for node, depth, dim in ((a, 1, p), (a | b, 2, q), (a | c, 2, r), (7, 3, r), (b, 3, p), (c, 3, p), (b | c, 4, p)):
        ARRIVE[p][node] = (depth, dim)
    for node, dim in ((a, q), (a, r), (a | b, r), (a | b, p), (a | c, p), (7, p)):
        FORWARD[dim][node] = 1 + ARRIVE[p][node][1]
KINDS = [sorted(set(ARRIVE[p][1:])) for p in range(3)]
ARRIVAL = [[0] + [1 + KINDS[p].index(kind) for kind in ARRIVE[p][1:]] for p in range(3)]

PARTS = 8
ROWS = 2
WORK = {4: (0,), 5: (1,), 6: (2,), 7: (3,), 8: (4,), 9: (5,), 10: (6,), 11: (7,)}
PLACE, PLACE_K, SOURCE, ARRIVED, OWNER, OCC, OCC_K, ALL_K, TRIP, SLAB, TABLE = 0, 3, 5, 14, 23, 26, 29, 31, 47, 48, 49

HBM = pl.BlockSpec(memory_space=pltpu.HBM)
SMEM = pl.BlockSpec(memory_space=pltpu.SMEM)
VMEM = pl.BlockSpec(memory_space=pltpu.VMEM)


def pick(values, index):
    found = jnp.int32(values[0])
    for n in range(1, len(values)):
        found = jnp.where(index == n, jnp.int32(values[n]), found)
    return found


def call(kernel, out_shape, operands, specs, out_specs=None, scratch=(), mib=46, cost=(0, 1 << 20), aliases=None):
    return pl.pallas_call(
        kernel,
        in_specs=list(specs),
        out_specs=out_specs,
        out_shape=out_shape,
        scratch_shapes=list(scratch),
        input_output_aliases=aliases or {},
        cost_estimate=pl.CostEstimate(flops=cost[0], bytes_accessed=cost[1], transcendentals=0),
        compiler_params=pltpu.CompilerParams(vmem_limit_bytes=mib * 2**20),
    )(*operands)


def f32(*shape):
    return jax.ShapeDtypeStruct(shape, jnp.float32)


def table_kernel(owner_ref, triples_ref, where_ref, out_ref):
    count = owner_ref.shape[0]
    trip = where_ref[0]
    out_ref[TRIP], out_ref[SLAB] = trip, where_ref[1]
    groups = triples_ref.shape[0] // 6

    def triple(m, g, n):
        return triples_ref[(m * groups + g) * 3 + n]

    def rank(occ):
        mine = owner_ref[occ]
        total = jnp.int32(0)
        for other in range(count):
            total += ((other < occ) & (owner_ref[other] == mine)).astype(jnp.int32)
        return total

    for x, occ in enumerate((triple(0, 0, 0), triple(0, 0, 1), triple(1, 0, 1))):
        owner = owner_ref[occ]
        rho = pick(CUBE, trip) ^ pick(CUBE, owner)
        out_ref[PLACE + x], out_ref[OWNER + x], out_ref[OCC + x] = rank(occ), owner, occ
        for n in range(3):
            out_ref[SOURCE + 3 * x + n] = pick(FORWARD[n], rho)
            out_ref[ARRIVED + 3 * x + n] = pick(ARRIVAL[n], rho)
    for m in range(2):
        occ = triple(m, trip, 2)
        out_ref[PLACE_K + m], out_ref[OCC_K + m] = rank(occ), occ
        for g in range(groups):
            out_ref[ALL_K + m * groups + g] = triple(m, g, 2)


def pairs_of(table_ref, groups, q_slab):
    found = [(m, PLACE_K + m, OCC, None) for m in range(2)]
    found += [(m, PLACE, OCC + 1 + m, OWNER) for m in range(2)]
    found += [(m, PLACE + 1 + m, ALL_K + m * groups + g, OWNER + 1 + m) for m in range(2) for g in range(groups)]
    pairs = []
    for m, row, col, plane in found:
        slab, q = lax.div(table_ref[col], q_slab), lax.rem(table_ref[col], q_slab)
        here = True if plane is None else table_ref[plane] == table_ref[TRIP]
        pairs.append((table_ref[row], slab, q, m * q_slab + q, here))
    return pairs


def thirds(size):
    height = -(-size // 24) * 8
    return height, (0, height, size - height)


def own_part(integrals_ref, table_ref, x, chunk, p, low=0):
    height, offsets = thirds(integrals_ref.shape[2])
    return integrals_ref.at[
        table_ref[PLACE + x], pl.ds(chunk * ROWS, ROWS), pl.ds(offsets[p] + low, height - low), :
    ]


def fetch(table_ref, integrals_ref, chunk, targets, sems):
    copies = []
    for d in range(3):
        for x in range(3):
            mine = pltpu.make_async_copy(
                own_part(integrals_ref, table_ref, x, chunk, d), targets[d].at[x], sems.at[3 * d + x]
            )
            needed = table_ref[SOURCE + 3 * x + d] == 0
            pl.when(needed)(mine.start)
            copies.append((needed, mine))
    return copies


def send_kernel(chunk, n_got, n_own, table_ref, *refs):
    got, own, rest = refs[:n_got], refs[n_got : n_got + n_own], refs[n_got + n_own :]
    copies = []
    if chunk is not None and not own:
        integrals_ref, *sent, sems = rest
        copies = fetch(table_ref, integrals_ref, chunk, sent, sems)
    else:
        sent = rest
    for d in range(3):
        for x in range(3):
            source = table_ref[SOURCE + 3 * x + d]
            for e, ref in enumerate((*own[d : d + 1], *got)):

                @pl.when(source == e + 1 - len(own[d : d + 1]))
                def _():
                    sent[d][x] = got[e - len(own[d : d + 1])][x] if e >= len(own[d : d + 1]) else ref[x]

    for needed, copy in copies:
        pl.when(needed)(copy.wait)


def payload(integrals):
    size = integrals.shape[-1]
    return f32(3, ROWS, thirds(size)[0], size)


def send(chunk, table, integrals, got, own):
    shape = payload(integrals)
    reads = chunk is not None and not own
    return call(
        lambda *refs: send_kernel(chunk, len(got), len(own), *refs),
        (shape,) * 3,
        (table, *got, *own) + ((integrals,) if reads else ()),
        (SMEM,) + (VMEM,) * (len(got) + len(own)) + ((HBM,) if reads else ()),
        (VMEM,) * 3,
        (pltpu.SemaphoreType.DMA((9,)),) if reads else (),
        cost=(0, 6 * 4 * shape.size),
        mib=46 if got else 49,
    )


def split(value):
    high = value.astype(jnp.bfloat16)
    return high, (value - high.astype(jnp.float32)).astype(jnp.bfloat16)


def product(highs, lows, block, dims):
    size, count = highs[0].shape[0], len(highs)

    def dot(parts, right):
        left = parts[0] if len(parts) == 1 else jnp.concatenate(parts)
        return lax.dot_general(left, right, (dims, ((), ())), preferred_element_type=jnp.float32)

    both, rest = dot(highs + lows, block[0]), dot(highs, block[1])
    part = lambda value, n: value[n * size : (n + 1) * size]
    return [part(both, n) + part(both, count + n) + part(rest, n) for n in range(count)]


def rows_kernel(chunks, first, last, ahead, table_ref, occ_ref, vir_c_ref, vir_a_ref, vir_b_ref, high_ref, low_ref, integrals_ref, *refs):
    count = 3 * (len(chunks) + 3)
    got, rest = refs[:count], refs[count:]
    if not first:
        in_ref, rest = rest[0], rest[1:]
    if last:
        keep_ref, give_ref, w_ref, k_ref, sems, out_ref = rest
    else:
        out_ref, rest = rest[0], rest[1:]
        if ahead is not None:
            own, own_sems, rest = rest[:3], rest[-1], rest[3:-1]
        w_ref, k_ref, sems = rest
    size = w_ref.shape[-1]
    height, offsets = thirds(size)

    copies = []
    for n, chunk in enumerate(chunks):
        for m in range(2):
            source = integrals_ref.at[table_ref[PLACE_K + m], pl.ds(chunk * ROWS, ROWS)]
            mine = pltpu.make_async_copy(source, k_ref.at[n, m], sems.at[n, 9 + m])
            mine.start()
            copies.append(mine)
        for x in range(3):
            for p in range(3):
                low = offsets[1] + height - offsets[2] if p == 2 else 0
                target = w_ref.at[n, x, :, pl.ds(offsets[p] + low, height - low), :]
                sem = sems.at[n, 3 * x + p]
                arrived = table_ref[ARRIVED + 3 * x + p]
                mine = pltpu.make_async_copy(own_part(integrals_ref, table_ref, x, chunk, p, low), target, sem)
                pl.when(arrived == 0)(mine.start)
                for kind, (depth, dim) in enumerate(KINDS[p]):
                    source = got[3 * (n + depth - 1) + dim].at[x, :, pl.ds(low, height - low), :]
                    pl.when(arrived == 1 + kind)(pltpu.make_async_copy(source, target, sem).start)
                copies.append(mine)
    own_copies = [] if ahead is None else fetch(table_ref, integrals_ref, ahead, own, own_sems)
    out_ref[...] = jnp.zeros_like(out_ref) if first else in_ref[...]
    virs = vir_a_ref[...] + vir_b_ref[...]
    shift_ij = [occ_ref[table_ref[OCC]] + occ_ref[table_ref[OCC + 1 + m]] for m in range(2)]
    shifts = [shift_ij[m] + occ_ref[table_ref[OCC_K + m]] for m in range(2)]
    for copy in copies:
        copy.wait()

    @pl.loop(0, len(chunks) * ROWS, unroll=True)
    def _(step):
        n, row = lax.div(step, ROWS), lax.rem(step, ROWS)
        c = table_ref[SLAB] * integrals_ref.shape[1] + chunks[0] * ROWS + step
        shared = [split(w_ref[n, x, row]) for x in range(3)]
        blocks = [[split(k_ref[n, m, row]) for m in range(2)], [shared[0]], [shared[1], shared[2]]]

        def against(highs, lows, dims):
            found = []
            for b in range(3):
                if len(blocks[b]) == 1:
                    found.append(product([highs(m, b) for m in range(2)], [lows(m, b) for m in range(2)], blocks[b][0], dims))
                else:
                    found.append([product([highs(m, b)], [lows(m, b)], blocks[b][m], dims)[0] for m in range(2)])
            return found

        terms = against(lambda m, b: high_ref[m, b], lambda m, b: low_ref[m, b], ((1,), (0,)))
        amps = []
        for m in range(2):
            connected = terms[0][m] + terms[1][m] + terms[2][m]
            amps.append(split(connected / (shifts[m] - (virs + vir_c_ref[c]))))
        terms = against(lambda m, b: amps[m][0], lambda m, b: amps[m][1], ((1,), (1,)))
        for m in range(2):
            for b in range(3):
                out_ref[:, m, :, b * size : (b + 1) * size] += terms[b][m].reshape(out_ref.shape[0], -1, size)

    for needed, copy in own_copies:
        pl.when(needed)(copy.wait)
    if last:
        core = lax.rem(table_ref[SLAB], 2)
        for chip in range(keep_ref.shape[0]):
            keep_ref[chip] = out_ref[2 * chip + core]
            give_ref[chip] = out_ref[2 * chip + 1 - core]


def rows(chunks, last, ahead, table, occ, vir, highs, lows, integrals, got, total):
    size, count = integrals.shape[-1], len(chunks)
    used = [buffer for step in got[chunks[0] : chunks[-1] + 4] for buffer in step]
    first = total is None
    operands = (table, occ, vir, vir[:, None], vir[None, :], highs, lows, integrals, *used) + (() if first else (total,))
    specs = (SMEM, SMEM, SMEM, VMEM, VMEM, VMEM, VMEM) + (HBM,) * (1 + len(used)) + (() if first else (VMEM,))
    shape = (2 * PARTS, 2, size // (2 * PARTS), 3 * size)
    half = f32(PARTS, *shape[1:])
    fetched = () if ahead is None else (payload(integrals),) * 3
    scratch = (
        pltpu.VMEM((count, 3, ROWS, size, size), jnp.float32),
        pltpu.VMEM((count, 2, ROWS, size, size), jnp.float32),
        pltpu.SemaphoreType.DMA((count, 11)),
    )
    return call(
        lambda *refs: rows_kernel(chunks, first, last, ahead, *refs),
        (half, half) if last else (f32(*shape),) + fetched,
        operands,
        specs,
        (VMEM, VMEM) if last else (VMEM,) * (1 + len(fetched)),
        scratch + ((pltpu.VMEM(shape, jnp.float32),) if last else (pltpu.SemaphoreType.DMA((9,)),) if fetched else ()),
        cost=(count * ROWS * 72 * size**3, count * ROWS * 20 * size**2 + 12 * 6 * size**2),
        mib=60 if first else 46,
    )


def to_slabs_kernel(table_ref, amplitudes_ref, out_ref, sems):
    copies = []
    for n, (row, slab, q, slot, here) in enumerate(pairs_of(table_ref, (sems.shape[0] - 4) // 2, amplitudes_ref.shape[1])):
        copy = pltpu.make_async_copy(amplitudes_ref.at[row, q], out_ref.at[:, slot], sems.at[n])
        mine = here & (slab == table_ref[SLAB])
        pl.when(mine)(copy.start)
        copies.append((mine, copy))
    for mine, copy in copies:
        pl.when(mine)(copy.wait)


def to_groups_kernel(q_slab, table_ref, by_slab_ref, ki_ref, out_ref):
    groups = out_ref.shape[0]
    parts = [(slab, slot) for _, slab, _, slot, _ in pairs_of(table_ref, groups, q_slab)]
    for m in range(2):
        ki_ref[m] = by_slab_ref[parts[m]]
        value = by_slab_ref[parts[2 + m]]
        for g in range(groups):
            out_ref[g, m] = by_slab_ref[parts[4 + m * groups + g]]
            out_ref[g, 2 + m] = value


def my_pairs_kernel(table_ref, ki_ref, by_trip_ref, out_ref):
    size = ki_ref.shape[-1]
    for m in range(2):
        pairs = (by_trip_ref[table_ref[OWNER], 2 + m], by_trip_ref[table_ref[OWNER + 1 + m], m], ki_ref[m])
        for chip in range(out_ref.shape[0]):
            for n, value in enumerate(pairs):
                out_ref[chip, m, :, n * size : (n + 1) * size] = value


def split_kernel(table_ref, mine_ref, other_ref, high_ref, low_ref):
    size = high_ref.shape[-1]
    core = lax.rem(table_ref[SLAB], 2)
    half = mine_ref.shape[2]
    for m in range(2):
        for n in range(3):
            for chip in range(mine_ref.shape[0]):
                for ref, parity in ((mine_ref, core), (other_ref, 1 - core)):
                    start = pl.multiple_of((2 * chip + parity) * half, half)
                    high, low = split(ref[chip, m, :, n * size : (n + 1) * size])
                    high_ref[m, n, pl.ds(start, half)] = high
                    low_ref[m, n, pl.ds(start, half)] = low


def sums_kernel(in_ref, ki_ref, out_ref):
    size = ki_ref.shape[-1]
    sums = jnp.sum(in_ref[...], axis=0)
    ki_ref[...] = sums[:, :, 2 * size :]
    for g in range(out_ref.shape[0]):
        out_ref[g, :2] = sums[:, :, size : 2 * size]
        out_ref[g, 2:] = sums[:, :, :size]


def from_groups_kernel(q_slab, table_ref, ki_ref, arrived_ref, out_ref):
    groups = arrived_ref.shape[0]
    for n, (_, slab, _, slot, here) in enumerate(pairs_of(table_ref, groups, q_slab)):

        @pl.when(here)
        def _():
            if n < 2:
                value = ki_ref[n]
            elif n < 4:
                value = jnp.sum(arrived_ref[:, n], axis=0)
            else:
                m, g = divmod(n - 4, groups)
                value = arrived_ref[g, m]
            out_ref[slab, slot] = value


def result_kernel(groups, table_ref, in_ref, out_ref):
    out_ref[...] = jnp.zeros_like(out_ref)
    for row, slab, q, slot, here in pairs_of(table_ref, groups, out_ref.shape[1]):

        @pl.when(here & (slab == table_ref[SLAB]))
        def _():
            out_ref[row, q] += in_ref[:, slot]


def on_device(integrals, amplitudes, occ_energy, vir_energy, owner, triples):
    n_slab, n_trip = lax.axis_size("slab"), lax.axis_size("trip")
    rows_count, q_slab, size = amplitudes.shape[:3]
    part = size // n_slab
    same_core = [list(range(core, n_slab, 2)) for core in range(2)]
    other_core = [(slab, slab ^ 1) for slab in range(n_slab)]
    where = jnp.stack([lax.axis_index("trip"), lax.axis_index("slab")]).astype(jnp.int32)
    table = call(
        table_kernel,
        jax.ShapeDtypeStruct((TABLE,), jnp.int32),
        (owner, triples.reshape(-1), where),
        (SMEM,) * 3,
        SMEM,
        cost=(0, 1 << 10),
    )
    amplitudes = amplitudes.reshape(rows_count, q_slab, n_slab, part, size)
    slots = 2 * q_slab

    chunks = integrals.shape[1] // ROWS
    got, total, pairs, parts = [], None, None, None
    own = ()
    for step in range(chunks + 3):
        previous = tuple(got[-1]) if got else ()
        if step == 2:
            by_slab = lax.all_to_all(to_slabs, "slab", 0, 0, tiled=True)
            t_ki, to_groups = call(
                lambda *refs: to_groups_kernel(q_slab, *refs),
                (f32(2, part, size), f32(n_trip, 4, part, size)),
                (table, by_slab),
                (SMEM, VMEM),
                (VMEM, VMEM),
                cost=(0, 32 * n_trip * part * size),
            )
            t_ki, to_groups, *previous = lax.optimization_barrier((t_ki, to_groups, *previous))
        if step == 3:
            by_trip = lax.all_to_all(to_groups, "trip", 0, 0, tiled=True)
            by_trip, *previous = lax.optimization_barrier((by_trip, *previous))
        if total is not None:
            total, *previous = lax.optimization_barrier((total, *previous))
        sent = send(step if step < chunks else None, table, integrals, previous, own)
        own = ()
        if step == 0:
            late_table, *sent = lax.optimization_barrier((table, *sent))
            to_slabs = call(
                to_slabs_kernel,
                f32(n_slab, slots, part, size),
                (late_table, amplitudes),
                (SMEM, HBM),
                VMEM,
                (pltpu.SemaphoreType.DMA((4 + 2 * n_trip,)),),
                cost=(0, 8 * slots * size**2),
            )
        if step == 3:
            by_trip, *sent = lax.optimization_barrier((by_trip, *sent))
            pairs = call(
                my_pairs_kernel,
                f32(PARTS, 2, part, 3 * size),
                (table, t_ki, by_trip),
                (SMEM, VMEM, VMEM),
                VMEM,
                cost=(0, 4 * 6 * size**2),
            )
            mine = lax.all_to_all(pairs, "slab", 0, 0, axis_index_groups=same_core, tiled=True)
        if step == 4:
            mine, *sent = lax.optimization_barrier((mine, *sent))
            other = lax.ppermute(mine, "slab", other_core)
            shape = jax.ShapeDtypeStruct((2, 3, size, size), jnp.bfloat16)
            parts = call(
                split_kernel,
                (shape, shape),
                (table, mine, other),
                (SMEM, VMEM, VMEM),
                (VMEM, VMEM),
                cost=(0, 16 * 6 * size**2),
            )
        got.append([lax.ppermute(sent[d], "trip", ALONG[d]) for d in range(3)])
        for key in (step,) if step < chunks + 2 else (step, step + 1):
            if key in WORK:
                last = key == chunks + 3
                ahead = step + 1 if step + 1 < chunks else None
                total, *own = rows(WORK[key], last, ahead, table, occ_energy, vir_energy, *parts, integrals, got, total)

    keep, give = total, *own
    give = lax.ppermute(give, "slab", other_core)
    by_slab = lax.all_to_all(keep + give, "slab", 0, 0, axis_index_groups=same_core, tiled=True)
    r_ki, outgoing = call(
        sums_kernel,
        (f32(2, part, size), f32(n_trip, 4, part, size)),
        (by_slab,),
        (VMEM,),
        (VMEM, VMEM),
    )
    arrived = lax.all_to_all(outgoing, "trip", 0, 0, tiled=True)
    to_slabs = call(
        lambda *refs: from_groups_kernel(q_slab, *refs),
        f32(n_slab, slots, part, size),
        (table, r_ki, arrived),
        (SMEM, VMEM, VMEM),
        VMEM,
    )
    result = call(
        lambda *refs: result_kernel(n_trip, *refs),
        f32(*amplitudes.shape),
        (table, lax.all_to_all(to_slabs, "slab", 0, 0, tiled=True)),
        (SMEM, VMEM),
        VMEM,
    )
    return result.reshape(rows_count, q_slab, size, size)


def solution(mesh):
    in_specs = (P("trip", "slab", None, None), P("trip", "slab", None, None), P(), P(), P(), P())
    out_specs = P("trip", "slab", None, None)
    return jax.shard_map(
        on_device, mesh=mesh, in_specs=in_specs, out_specs=out_specs, check_vma=False
    )
```

```python
import jax
import jax.numpy as jnp
from jax import lax
from jax.experimental import pallas as pl
from jax.experimental.pallas import tpu as pltpu
from jax.sharding import PartitionSpec as P

GRAY = (0, 1, 3, 2)
CUBE = tuple((t // 4) * 4 + GRAY[t % 4] for t in range(8))
FROM_CUBE = tuple(CUBE.index(v) for v in range(8))
ALONG = tuple([(t, FROM_CUBE[CUBE[t] ^ (1 << d)]) for t in range(8)] for d in range(3))

ARRIVE = [[None] * 8 for _ in range(3)]
FORWARD = [[0] * 8 for _ in range(3)]
for p in range(3):
    q, r = (p + 1) % 3, (p + 2) % 3
    a, b, c = 1 << p, 1 << q, 1 << r
    for node, depth, dim in ((a, 1, p), (a | b, 2, q), (a | c, 2, r), (7, 3, r), (b, 3, p), (c, 3, p), (b | c, 4, p)):
        ARRIVE[p][node] = (depth, dim)
    for node, dim in ((a, q), (a, r), (a | b, r), (a | b, p), (a | c, p), (7, p)):
        FORWARD[dim][node] = 1 + ARRIVE[p][node][1]
KINDS = [sorted(set(ARRIVE[p][1:])) for p in range(3)]
ARRIVAL = [[0] + [1 + KINDS[p].index(kind) for kind in ARRIVE[p][1:]] for p in range(3)]

PARTS = 8
ROWS = 2
WORK = {4: (0,), 5: (1,), 6: (2,), 7: (3,), 8: (4,), 9: (5,), 10: (6, 7)}
PLACE, PLACE_K, SOURCE, ARRIVED, OWNER, OCC, OCC_K, ALL_K, TRIP, SLAB, TABLE = 0, 3, 5, 14, 23, 26, 29, 31, 47, 48, 49

HBM = pl.BlockSpec(memory_space=pltpu.HBM)
SMEM = pl.BlockSpec(memory_space=pltpu.SMEM)
VMEM = pl.BlockSpec(memory_space=pltpu.VMEM)


def pick(values, index):
    found = jnp.int32(values[0])
    for n in range(1, len(values)):
        found = jnp.where(index == n, jnp.int32(values[n]), found)
    return found


def call(kernel, out_shape, operands, specs, out_specs=None, scratch=(), mib=46, cost=(0, 1 << 20), aliases=None):
    return pl.pallas_call(
        kernel,
        in_specs=list(specs),
        out_specs=out_specs,
        out_shape=out_shape,
        scratch_shapes=list(scratch),
        input_output_aliases=aliases or {},
        cost_estimate=pl.CostEstimate(flops=cost[0], bytes_accessed=cost[1], transcendentals=0),
        compiler_params=pltpu.CompilerParams(vmem_limit_bytes=mib * 2**20),
    )(*operands)


def f32(*shape):
    return jax.ShapeDtypeStruct(shape, jnp.float32)


def table_kernel(owner_ref, triples_ref, where_ref, out_ref):
    count = owner_ref.shape[0]
    trip = where_ref[0]
    out_ref[TRIP], out_ref[SLAB] = trip, where_ref[1]
    groups = triples_ref.shape[0] // 6

    def triple(m, g, n):
        return triples_ref[(m * groups + g) * 3 + n]

    def rank(occ):
        mine = owner_ref[occ]
        total = jnp.int32(0)
        for other in range(count):
            total += ((other < occ) & (owner_ref[other] == mine)).astype(jnp.int32)
        return total

    for x, occ in enumerate((triple(0, 0, 0), triple(0, 0, 1), triple(1, 0, 1))):
        owner = owner_ref[occ]
        rho = pick(CUBE, trip) ^ pick(CUBE, owner)
        out_ref[PLACE + x], out_ref[OWNER + x], out_ref[OCC + x] = rank(occ), owner, occ
        for n in range(3):
            out_ref[SOURCE + 3 * x + n] = pick(FORWARD[n], rho)
            out_ref[ARRIVED + 3 * x + n] = pick(ARRIVAL[n], rho)
    for m in range(2):
        occ = triple(m, trip, 2)
        out_ref[PLACE_K + m], out_ref[OCC_K + m] = rank(occ), occ
        for g in range(groups):
            out_ref[ALL_K + m * groups + g] = triple(m, g, 2)


def pairs_of(table_ref, groups, q_slab):
    found = [(m, PLACE_K + m, OCC, None) for m in range(2)]
    found += [(m, PLACE, OCC + 1 + m, OWNER) for m in range(2)]
    found += [(m, PLACE + 1 + m, ALL_K + m * groups + g, OWNER + 1 + m) for m in range(2) for g in range(groups)]
    pairs = []
    for m, row, col, plane in found:
        slab, q = lax.div(table_ref[col], q_slab), lax.rem(table_ref[col], q_slab)
        here = True if plane is None else table_ref[plane] == table_ref[TRIP]
        pairs.append((table_ref[row], slab, q, m * q_slab + q, here))
    return pairs


def thirds(size):
    height = -(-size // 24) * 8
    return height, (0, height, size - height)


def own_part(integrals_ref, table_ref, x, chunk, p, low=0):
    height, offsets = thirds(integrals_ref.shape[2])
    return integrals_ref.at[
        table_ref[PLACE + x], pl.ds(chunk * ROWS, ROWS), pl.ds(offsets[p] + low, height - low), :
    ]


def fetch(table_ref, integrals_ref, step, targets, sems):
    chunk = min(step, integrals_ref.shape[1] // ROWS - 1)
    copies = []
    for d in range(3):
        for x in range(3):
            mine = pltpu.make_async_copy(
                own_part(integrals_ref, table_ref, x, chunk, (d + 2 * (step - chunk)) % 3), targets[d].at[x], sems.at[3 * d + x]
            )
            needed = table_ref[SOURCE + 3 * x + d] == 0
            pl.when(needed)(mine.start)
            copies.append((needed, mine))
    return copies


def send_kernel(step, n_got, n_own, table_ref, *refs):
    got, own, rest = refs[:n_got], refs[n_got : n_got + n_own], refs[n_got + n_own :]
    copies = []
    if step is not None and not own:
        integrals_ref, *sent, sems = rest
        copies = fetch(table_ref, integrals_ref, step, sent, sems)
    else:
        sent = rest
    for d in range(3):
        for x in range(3):
            source = table_ref[SOURCE + 3 * x + d]
            for e, ref in enumerate((*own[d : d + 1], *got)):

                @pl.when(source == e + 1 - len(own[d : d + 1]))
                def _():
                    sent[d][x] = got[e - len(own[d : d + 1])][x] if e >= len(own[d : d + 1]) else ref[x]

    for needed, copy in copies:
        pl.when(needed)(copy.wait)


def payload(integrals):
    size = integrals.shape[-1]
    return f32(3, ROWS, thirds(size)[0], size)


def send(step, table, integrals, got, own):
    shape = payload(integrals)
    reads = step is not None and not own
    return call(
        lambda *refs: send_kernel(step, len(got), len(own), *refs),
        (shape,) * 3,
        (table, *got, *own) + ((integrals,) if reads else ()),
        (SMEM,) + (VMEM,) * (len(got) + len(own)) + ((HBM,) if reads else ()),
        (VMEM,) * 3,
        (pltpu.SemaphoreType.DMA((9,)),) if reads else (),
        cost=(0, 6 * 4 * shape.size),
        mib=46 if got else 49,
    )


def split(value):
    high = value.astype(jnp.bfloat16)
    return high, (value - high.astype(jnp.float32)).astype(jnp.bfloat16)


def product(highs, lows, block, dims):
    size, count = highs[0].shape[0], len(highs)

    def dot(parts, right):
        left = parts[0] if len(parts) == 1 else jnp.concatenate(parts)
        return lax.dot_general(left, right, (dims, ((), ())), preferred_element_type=jnp.float32)

    both, rest = dot(highs + lows, block[0]), dot(highs, block[1])
    part = lambda value, n: value[n * size : (n + 1) * size]
    return [part(both, n) + part(both, count + n) + part(rest, n) for n in range(count)]


def rows_kernel(chunks, first, last, ahead, table_ref, occ_ref, vir_c_ref, vir_a_ref, vir_b_ref, high_ref, low_ref, integrals_ref, *refs):
    count = 3 * (len(chunks) + (2 if last else 3))
    got, rest = refs[:count], refs[count:]
    if not first:
        in_ref, rest = rest[0], rest[1:]
    if last:
        keep_ref, give_ref, w_ref, k_ref, sems, out_ref = rest
    else:
        out_ref, rest = rest[0], rest[1:]
        if ahead is not None:
            own, own_sems, rest = rest[:3], rest[-1], rest[3:-1]
        w_ref, k_ref, sems = rest
    size = w_ref.shape[-1]
    height, offsets = thirds(size)

    copies = []
    for n, chunk in enumerate(chunks):
        for m in range(2):
            source = integrals_ref.at[table_ref[PLACE_K + m], pl.ds(chunk * ROWS, ROWS)]
            mine = pltpu.make_async_copy(source, k_ref.at[n, m], sems.at[n, 9 + m])
            mine.start()
            copies.append(mine)
        for x in range(3):
            for p in range(3):
                low = offsets[1] + height - offsets[2] if p == 2 else 0
                target = w_ref.at[n, x, :, pl.ds(offsets[p] + low, height - low), :]
                sem = sems.at[n, 3 * x + p]
                arrived = table_ref[ARRIVED + 3 * x + p]
                mine = pltpu.make_async_copy(own_part(integrals_ref, table_ref, x, chunk, p, low), target, sem)
                pl.when(arrived == 0)(mine.start)
                for kind, (depth, dim) in enumerate(KINDS[p]):
                    if depth == 4 and last and n == len(chunks) - 1:
                        depth, dim = 3, (p + 2) % 3
                    source = got[3 * (n + depth - 1) + dim].at[x, :, pl.ds(low, height - low), :]
                    pl.when(arrived == 1 + kind)(pltpu.make_async_copy(source, target, sem).start)
                copies.append(mine)
    own_copies = [] if ahead is None else fetch(table_ref, integrals_ref, ahead, own, own_sems)
    out_ref[...] = jnp.zeros_like(out_ref) if first else in_ref[...]
    virs = vir_a_ref[...] + vir_b_ref[...]
    shift_ij = [occ_ref[table_ref[OCC]] + occ_ref[table_ref[OCC + 1 + m]] for m in range(2)]
    shifts = [shift_ij[m] + occ_ref[table_ref[OCC_K + m]] for m in range(2)]
    for copy in copies:
        copy.wait()

    @pl.loop(0, len(chunks) * ROWS, unroll=True)
    def _(step):
        n, row = lax.div(step, ROWS), lax.rem(step, ROWS)
        c = table_ref[SLAB] * integrals_ref.shape[1] + chunks[0] * ROWS + step
        shared = [split(w_ref[n, x, row]) for x in range(3)]
        blocks = [[split(k_ref[n, m, row]) for m in range(2)], [shared[0]], [shared[1], shared[2]]]

        def against(highs, lows, dims):
            found = []
            for b in range(3):
                if len(blocks[b]) == 1:
                    found.append(product([highs(m, b) for m in range(2)], [lows(m, b) for m in range(2)], blocks[b][0], dims))
                else:
                    found.append([product([highs(m, b)], [lows(m, b)], blocks[b][m], dims)[0] for m in range(2)])
            return found

        terms = against(lambda m, b: high_ref[m, b], lambda m, b: low_ref[m, b], ((1,), (0,)))
        amps = []
        for m in range(2):
            connected = terms[0][m] + terms[1][m] + terms[2][m]
            amps.append(split(connected / (shifts[m] - (virs + vir_c_ref[c]))))
        terms = against(lambda m, b: amps[m][0], lambda m, b: amps[m][1], ((1,), (1,)))
        for m in range(2):
            for b in range(3):
                out_ref[:, m, :, b * size : (b + 1) * size] += terms[b][m].reshape(out_ref.shape[0], -1, size)

    for needed, copy in own_copies:
        pl.when(needed)(copy.wait)
    if last:
        core = lax.rem(table_ref[SLAB], 2)
        for chip in range(keep_ref.shape[0]):
            keep_ref[chip] = out_ref[2 * chip + core]
            give_ref[chip] = out_ref[2 * chip + 1 - core]


def rows(chunks, last, ahead, table, occ, vir, highs, lows, integrals, got, total):
    size, count = integrals.shape[-1], len(chunks)
    used = [buffer for step in got[chunks[0] : chunks[-1] + 4] for buffer in step]
    first = total is None
    operands = (table, occ, vir, vir[:, None], vir[None, :], highs, lows, integrals, *used) + (() if first else (total,))
    specs = (SMEM, SMEM, SMEM, VMEM, VMEM, VMEM, VMEM) + (HBM,) * (1 + len(used)) + (() if first else (VMEM,))
    shape = (2 * PARTS, 2, size // (2 * PARTS), 3 * size)
    half = f32(PARTS, *shape[1:])
    fetched = () if ahead is None else (payload(integrals),) * 3
    scratch = (
        pltpu.VMEM((count, 3, ROWS, size, size), jnp.float32),
        pltpu.VMEM((count, 2, ROWS, size, size), jnp.float32),
        pltpu.SemaphoreType.DMA((count, 11)),
    )
    return call(
        lambda *refs: rows_kernel(chunks, first, last, ahead, *refs),
        (half, half) if last else (f32(*shape),) + fetched,
        operands,
        specs,
        (VMEM, VMEM) if last else (VMEM,) * (1 + len(fetched)),
        scratch + ((pltpu.VMEM(shape, jnp.float32),) if last else (pltpu.SemaphoreType.DMA((9,)),) if fetched else ()),
        cost=(count * ROWS * 72 * size**3, count * ROWS * 20 * size**2 + 12 * 6 * size**2),
        mib=60 if first else 46,
    )


def to_slabs_kernel(table_ref, amplitudes_ref, out_ref, sems):
    copies = []
    for n, (row, slab, q, slot, here) in enumerate(pairs_of(table_ref, (sems.shape[0] - 4) // 2, amplitudes_ref.shape[1])):
        copy = pltpu.make_async_copy(amplitudes_ref.at[row, q], out_ref.at[:, slot], sems.at[n])
        mine = here & (slab == table_ref[SLAB])
        pl.when(mine)(copy.start)
        copies.append((mine, copy))
    for mine, copy in copies:
        pl.when(mine)(copy.wait)


def to_groups_kernel(q_slab, table_ref, by_slab_ref, ki_ref, out_ref):
    groups = out_ref.shape[0]
    parts = [(slab, slot) for _, slab, _, slot, _ in pairs_of(table_ref, groups, q_slab)]
    for m in range(2):
        ki_ref[m] = by_slab_ref[parts[m]]
        value = by_slab_ref[parts[2 + m]]
        for g in range(groups):
            out_ref[g, m] = by_slab_ref[parts[4 + m * groups + g]]
            out_ref[g, 2 + m] = value


def my_pairs_kernel(table_ref, ki_ref, by_trip_ref, out_ref):
    size = ki_ref.shape[-1]
    for m in range(2):
        pairs = (by_trip_ref[table_ref[OWNER], 2 + m], by_trip_ref[table_ref[OWNER + 1 + m], m], ki_ref[m])
        for chip in range(out_ref.shape[0]):
            for n, value in enumerate(pairs):
                out_ref[chip, m, :, n * size : (n + 1) * size] = value


def split_kernel(table_ref, mine_ref, other_ref, high_ref, low_ref):
    size = high_ref.shape[-1]
    core = lax.rem(table_ref[SLAB], 2)
    half = mine_ref.shape[2]
    for m in range(2):
        for n in range(3):
            for chip in range(mine_ref.shape[0]):
                for ref, parity in ((mine_ref, core), (other_ref, 1 - core)):
                    start = pl.multiple_of((2 * chip + parity) * half, half)
                    high, low = split(ref[chip, m, :, n * size : (n + 1) * size])
                    high_ref[m, n, pl.ds(start, half)] = high
                    low_ref[m, n, pl.ds(start, half)] = low


def sums_kernel(in_ref, ki_ref, out_ref):
    size = ki_ref.shape[-1]
    sums = jnp.sum(in_ref[...], axis=0)
    ki_ref[...] = sums[:, :, 2 * size :]
    for g in range(out_ref.shape[0]):
        out_ref[g, :2] = sums[:, :, size : 2 * size]
        out_ref[g, 2:] = sums[:, :, :size]


def from_groups_kernel(q_slab, table_ref, ki_ref, arrived_ref, out_ref):
    groups = arrived_ref.shape[0]
    for n, (_, slab, _, slot, here) in enumerate(pairs_of(table_ref, groups, q_slab)):

        @pl.when(here)
        def _():
            if n < 2:
                value = ki_ref[n]
            elif n < 4:
                value = jnp.sum(arrived_ref[:, n], axis=0)
            else:
                m, g = divmod(n - 4, groups)
                value = arrived_ref[g, m]
            out_ref[slab, slot] = value


def result_kernel(groups, table_ref, in_ref, out_ref):
    out_ref[...] = jnp.zeros_like(out_ref)
    for row, slab, q, slot, here in pairs_of(table_ref, groups, out_ref.shape[1]):

        @pl.when(here & (slab == table_ref[SLAB]))
        def _():
            out_ref[row, q] += in_ref[:, slot]


def on_device(integrals, amplitudes, occ_energy, vir_energy, owner, triples):
    n_slab, n_trip = lax.axis_size("slab"), lax.axis_size("trip")
    rows_count, q_slab, size = amplitudes.shape[:3]
    part = size // n_slab
    same_core = [list(range(core, n_slab, 2)) for core in range(2)]
    other_core = [(slab, slab ^ 1) for slab in range(n_slab)]
    where = jnp.stack([lax.axis_index("trip"), lax.axis_index("slab")]).astype(jnp.int32)
    table = call(
        table_kernel,
        jax.ShapeDtypeStruct((TABLE,), jnp.int32),
        (owner, triples.reshape(-1), where),
        (SMEM,) * 3,
        SMEM,
        cost=(0, 1 << 10),
    )
    amplitudes = amplitudes.reshape(rows_count, q_slab, n_slab, part, size)
    slots = 2 * q_slab

    chunks = integrals.shape[1] // ROWS
    got, total, pairs, parts = [], None, None, None
    own = ()
    for step in range(chunks + 2):
        previous = tuple(got[-1]) if got else ()
        if step == 2:
            by_slab = lax.all_to_all(to_slabs, "slab", 0, 0, tiled=True)
            t_ki, to_groups = call(
                lambda *refs: to_groups_kernel(q_slab, *refs),
                (f32(2, part, size), f32(n_trip, 4, part, size)),
                (table, by_slab),
                (SMEM, VMEM),
                (VMEM, VMEM),
                cost=(0, 32 * n_trip * part * size),
            )
            t_ki, to_groups, *previous = lax.optimization_barrier((t_ki, to_groups, *previous))
        if step == 3:
            by_trip = lax.all_to_all(to_groups, "trip", 0, 0, tiled=True)
            by_trip, *previous = lax.optimization_barrier((by_trip, *previous))
        if total is not None:
            total, *previous = lax.optimization_barrier((total, *previous))
        sent = send(step if step <= chunks else None, table, integrals, previous, own)
        own = ()
        if step == 0:
            late_table, *sent = lax.optimization_barrier((table, *sent))
            to_slabs = call(
                to_slabs_kernel,
                f32(n_slab, slots, part, size),
                (late_table, amplitudes),
                (SMEM, HBM),
                VMEM,
                (pltpu.SemaphoreType.DMA((4 + 2 * n_trip,)),),
                cost=(0, 8 * slots * size**2),
            )
        if step == 3:
            by_trip, *sent = lax.optimization_barrier((by_trip, *sent))
            pairs = call(
                my_pairs_kernel,
                f32(PARTS, 2, part, 3 * size),
                (table, t_ki, by_trip),
                (SMEM, VMEM, VMEM),
                VMEM,
                cost=(0, 4 * 6 * size**2),
            )
            mine = lax.all_to_all(pairs, "slab", 0, 0, axis_index_groups=same_core, tiled=True)
        if step == 4:
            mine, *sent = lax.optimization_barrier((mine, *sent))
            other = lax.ppermute(mine, "slab", other_core)
            shape = jax.ShapeDtypeStruct((2, 3, size, size), jnp.bfloat16)
            parts = call(
                split_kernel,
                (shape, shape),
                (table, mine, other),
                (SMEM, VMEM, VMEM),
                (VMEM, VMEM),
                cost=(0, 16 * 6 * size**2),
            )
        got.append([lax.ppermute(sent[d], "trip", ALONG[d]) for d in range(3)])
        for key in (step,) if step < chunks + 1 else (step, step + 1):
            if key in WORK:
                last = key == chunks + 2
                ahead = step + 1 if step < chunks else None
                total, *own = rows(WORK[key], last, ahead, table, occ_energy, vir_energy, *parts, integrals, got, total)

    keep, give = total, *own
    give = lax.ppermute(give, "slab", other_core)
    by_slab = lax.all_to_all(keep + give, "slab", 0, 0, axis_index_groups=same_core, tiled=True)
    r_ki, outgoing = call(
        sums_kernel,
        (f32(2, part, size), f32(n_trip, 4, part, size)),
        (by_slab,),
        (VMEM,),
        (VMEM, VMEM),
    )
    arrived = lax.all_to_all(outgoing, "trip", 0, 0, tiled=True)
    to_slabs = call(
        lambda *refs: from_groups_kernel(q_slab, *refs),
        f32(n_slab, slots, part, size),
        (table, r_ki, arrived),
        (SMEM, VMEM, VMEM),
        VMEM,
    )
    result = call(
        lambda *refs: result_kernel(n_trip, *refs),
        f32(*amplitudes.shape),
        (table, lax.all_to_all(to_slabs, "slab", 0, 0, tiled=True)),
        (SMEM, VMEM),
        VMEM,
    )
    return result.reshape(rows_count, q_slab, size, size)


def solution(mesh):
    in_specs = (P("trip", "slab", None, None), P("trip", "slab", None, None), P(), P(), P(), P())
    out_specs = P("trip", "slab", None, None)
    return jax.shard_map(
        on_device, mesh=mesh, in_specs=in_specs, out_specs=out_specs, check_vma=False
    )
```

```python
import jax
import jax.numpy as jnp
from jax import lax
from jax.experimental import pallas as pl
from jax.experimental.pallas import tpu as pltpu
from jax.sharding import PartitionSpec as P

GRAY = (0, 1, 3, 2)
CUBE = tuple((t // 4) * 4 + GRAY[t % 4] for t in range(8))
FROM_CUBE = tuple(CUBE.index(v) for v in range(8))
ALONG = tuple([(t, FROM_CUBE[CUBE[t] ^ (1 << d)]) for t in range(8)] for d in range(3))

ARRIVE = [[None] * 8 for _ in range(3)]
FORWARD = [[0] * 8 for _ in range(3)]
for p in range(3):
    q, r = (p + 1) % 3, (p + 2) % 3
    a, b, c = 1 << p, 1 << q, 1 << r
    for node, depth, dim in ((a, 1, p), (a | b, 2, q), (a | c, 2, r), (7, 3, r), (b, 3, p), (c, 3, p), (b | c, 4, p)):
        ARRIVE[p][node] = (depth, dim)
    for node, dim in ((a, q), (a, r), (a | b, r), (a | b, p), (a | c, p), (7, p)):
        FORWARD[dim][node] = 1 + ARRIVE[p][node][1]
KINDS = [sorted(set(ARRIVE[p][1:])) for p in range(3)]
ARRIVAL = [[0] + [1 + KINDS[p].index(kind) for kind in ARRIVE[p][1:]] for p in range(3)]

PARTS = 8
ROWS = 2
WORK = {4: (0,), 5: (1,), 6: (2,), 7: (3,), 8: (4,), 9: (5,), 10: (6, 7)}
PLACE, PLACE_K, SOURCE, ARRIVED, OWNER, OCC, OCC_K, ALL_K, TRIP, SLAB, TABLE = 0, 3, 5, 14, 23, 26, 29, 31, 47, 48, 49

HBM = pl.BlockSpec(memory_space=pltpu.HBM)
SMEM = pl.BlockSpec(memory_space=pltpu.SMEM)
VMEM = pl.BlockSpec(memory_space=pltpu.VMEM)


def pick(values, index):
    found = jnp.int32(values[0])
    for n in range(1, len(values)):
        found = jnp.where(index == n, jnp.int32(values[n]), found)
    return found


def call(kernel, out_shape, operands, specs, out_specs=None, scratch=(), mib=46, cost=(0, 1 << 20), aliases=None):
    return pl.pallas_call(
        kernel,
        in_specs=list(specs),
        out_specs=out_specs,
        out_shape=out_shape,
        scratch_shapes=list(scratch),
        input_output_aliases=aliases or {},
        cost_estimate=pl.CostEstimate(flops=cost[0], bytes_accessed=cost[1], transcendentals=0),
        compiler_params=pltpu.CompilerParams(vmem_limit_bytes=mib * 2**20),
    )(*operands)


def f32(*shape):
    return jax.ShapeDtypeStruct(shape, jnp.float32)


def table_kernel(owner_ref, triples_ref, where_ref, out_ref):
    count = owner_ref.shape[0]
    trip = where_ref[0]
    out_ref[TRIP], out_ref[SLAB] = trip, where_ref[1]
    groups = triples_ref.shape[0] // 6

    def triple(m, g, n):
        return triples_ref[(m * groups + g) * 3 + n]

    def rank(occ):
        mine = owner_ref[occ]
        total = jnp.int32(0)
        for other in range(count):
            total += ((other < occ) & (owner_ref[other] == mine)).astype(jnp.int32)
        return total

    for x, occ in enumerate((triple(0, 0, 0), triple(0, 0, 1), triple(1, 0, 1))):
        owner = owner_ref[occ]
        rho = pick(CUBE, trip) ^ pick(CUBE, owner)
        out_ref[PLACE + x], out_ref[OWNER + x], out_ref[OCC + x] = rank(occ), owner, occ
        for n in range(3):
            out_ref[SOURCE + 3 * x + n] = pick(FORWARD[n], rho)
            out_ref[ARRIVED + 3 * x + n] = pick(ARRIVAL[n], rho)
    for m in range(2):
        occ = triple(m, trip, 2)
        out_ref[PLACE_K + m], out_ref[OCC_K + m] = rank(occ), occ
        for g in range(groups):
            out_ref[ALL_K + m * groups + g] = triple(m, g, 2)


def pairs_of(table_ref, groups, q_slab):
    found = [(m, PLACE_K + m, OCC, None) for m in range(2)]
    found += [(m, PLACE, OCC + 1 + m, OWNER) for m in range(2)]
    found += [(m, PLACE + 1 + m, ALL_K + m * groups + g, OWNER + 1 + m) for m in range(2) for g in range(groups)]
    pairs = []
    for m, row, col, plane in found:
        slab, q = lax.div(table_ref[col], q_slab), lax.rem(table_ref[col], q_slab)
        here = True if plane is None else table_ref[plane] == table_ref[TRIP]
        pairs.append((table_ref[row], slab, q, m * q_slab + q, here))
    return pairs


def thirds(size):
    height = -(-size // 24) * 8
    return height, (0, height, size - height)


def own_part(integrals_ref, table_ref, x, chunk, p, low=0):
    height, offsets = thirds(integrals_ref.shape[2])
    return integrals_ref.at[
        table_ref[PLACE + x], pl.ds(chunk * ROWS, ROWS), pl.ds(offsets[p] + low, height - low), :
    ]


def fetch(table_ref, integrals_ref, step, targets, sems):
    chunk = min(step, integrals_ref.shape[1] // ROWS - 1)
    copies = []
    for d in range(3):
        for x in range(3):
            mine = pltpu.make_async_copy(
                own_part(integrals_ref, table_ref, x, chunk, (d + 2 * (step - chunk)) % 3), targets[d].at[x], sems.at[3 * d + x]
            )
            needed = table_ref[SOURCE + 3 * x + d] == 0
            pl.when(needed)(mine.start)
            copies.append((needed, mine))
    return copies


def send_kernel(step, n_got, n_own, table_ref, *refs):
    got, own, rest = refs[:n_got], refs[n_got : n_got + n_own], refs[n_got + n_own :]
    copies = []
    if step is not None and not own:
        integrals_ref, *sent, sems = rest
        copies = fetch(table_ref, integrals_ref, step, sent, sems)
    else:
        sent = rest
    for d in range(3):
        for x in range(3):
            source = table_ref[SOURCE + 3 * x + d]
            for e, ref in enumerate((*own[d : d + 1], *got)):

                @pl.when(source == e + 1 - len(own[d : d + 1]))
                def _():
                    sent[d][x] = got[e - len(own[d : d + 1])][x] if e >= len(own[d : d + 1]) else ref[x]

    for needed, copy in copies:
        pl.when(needed)(copy.wait)


def payload(integrals):
    size = integrals.shape[-1]
    return f32(3, ROWS, thirds(size)[0], size)


def send(step, table, integrals, got, own):
    shape = payload(integrals)
    reads = step is not None and not own
    return call(
        lambda *refs: send_kernel(step, len(got), len(own), *refs),
        (shape,) * 3,
        (table, *got, *own) + ((integrals,) if reads else ()),
        (SMEM,) + (VMEM,) * (len(got) + len(own)) + ((HBM,) if reads else ()),
        (VMEM,) * 3,
        (pltpu.SemaphoreType.DMA((9,)),) if reads else (),
        cost=(0, 6 * 4 * shape.size),
        mib=46 if got else 49,
    )


def split(value):
    high = value.astype(jnp.bfloat16)
    return high, (value - high.astype(jnp.float32)).astype(jnp.bfloat16)


def product(highs, lows, block, dims):
    size, count = highs[0].shape[0], len(highs)

    def dot(parts, right):
        left = parts[0] if len(parts) == 1 else jnp.concatenate(parts)
        return lax.dot_general(left, right, (dims, ((), ())), preferred_element_type=jnp.float32)

    both, rest = dot(highs + lows, block[0]), dot(highs, block[1])
    part = lambda value, n: value[n * size : (n + 1) * size]
    return [part(both, n) + part(both, count + n) + part(rest, n) for n in range(count)]


def rows_kernel(chunks, first, last, ahead, table_ref, occ_ref, vir_c_ref, vir_a_ref, vir_b_ref, high_ref, low_ref, integrals_ref, *refs):
    count = 3 * (len(chunks) + (2 if last else 3))
    got, rest = refs[:count], refs[count:]
    if not first:
        in_ref, rest = rest[0], rest[1:]
    if last:
        keep_ref, give_ref, w_ref, k_ref, sems, out_ref = rest
    else:
        out_ref, rest = rest[0], rest[1:]
        if ahead is not None:
            own, own_sems, rest = rest[:3], rest[-1], rest[3:-1]
        w_ref, k_ref, sems = rest
    size = w_ref.shape[-1]
    height, offsets = thirds(size)

    copies = []
    for n, chunk in enumerate(chunks):
        for m in range(2):
            source = integrals_ref.at[table_ref[PLACE_K + m], pl.ds(chunk * ROWS, ROWS)]
            mine = pltpu.make_async_copy(source, k_ref.at[n, m], sems.at[n, 9 + m])
            mine.start()
            copies.append(mine)
        for x in range(3):
            for p in range(3):
                low = offsets[1] + height - offsets[2] if p == 2 else 0
                target = w_ref.at[n, x, :, pl.ds(offsets[p] + low, height - low), :]
                sem = sems.at[n, 3 * x + p]
                arrived = table_ref[ARRIVED + 3 * x + p]
                mine = pltpu.make_async_copy(own_part(integrals_ref, table_ref, x, chunk, p, low), target, sem)
                pl.when(arrived == 0)(mine.start)
                for kind, (depth, dim) in enumerate(KINDS[p]):
                    if depth == 4 and last and n == len(chunks) - 1:
                        depth, dim = 3, (p + 2) % 3
                    source = got[3 * (n + depth - 1) + dim].at[x, :, pl.ds(low, height - low), :]
                    pl.when(arrived == 1 + kind)(pltpu.make_async_copy(source, target, sem).start)
                copies.append(mine)
    own_copies = [] if ahead is None else fetch(table_ref, integrals_ref, ahead, own, own_sems)
    out_ref[...] = jnp.zeros_like(out_ref) if first else in_ref[...]
    virs = vir_a_ref[...] + vir_b_ref[...]
    shift_ij = [occ_ref[table_ref[OCC]] + occ_ref[table_ref[OCC + 1 + m]] for m in range(2)]
    shifts = [shift_ij[m] + occ_ref[table_ref[OCC_K + m]] for m in range(2)]
    for copy in copies:
        copy.wait()

    @pl.loop(0, len(chunks) * ROWS, unroll=True)
    def _(step):
        n, row = lax.div(step, ROWS), lax.rem(step, ROWS)
        c = table_ref[SLAB] * integrals_ref.shape[1] + chunks[0] * ROWS + step
        shared = [split(w_ref[n, x, row]) for x in range(3)]
        blocks = [[split(k_ref[n, m, row]) for m in range(2)], [shared[0]], [shared[1], shared[2]]]

        def against(highs, lows, dims):
            found = []
            for b in range(3):
                if len(blocks[b]) == 1:
                    found.append(product([highs(m, b) for m in range(2)], [lows(m, b) for m in range(2)], blocks[b][0], dims))
                else:
                    found.append([product([highs(m, b)], [lows(m, b)], blocks[b][m], dims)[0] for m in range(2)])
            return found

        terms = against(lambda m, b: high_ref[m, b], lambda m, b: low_ref[m, b], ((1,), (0,)))
        amps = []
        for m in range(2):
            connected = terms[0][m] + terms[1][m] + terms[2][m]
            amps.append(split(connected / (shifts[m] - (virs + vir_c_ref[c]))))
        terms = against(lambda m, b: amps[m][0], lambda m, b: amps[m][1], ((1,), (1,)))
        for m in range(2):
            for b in range(3):
                out_ref[:, m, :, b * size : (b + 1) * size] += terms[b][m].reshape(out_ref.shape[0], -1, size)

    for needed, copy in own_copies:
        pl.when(needed)(copy.wait)
    if last:
        core = lax.rem(table_ref[SLAB], 2)
        for chip in range(keep_ref.shape[0]):
            keep_ref[chip] = out_ref[2 * chip + core]
            give_ref[chip] = out_ref[2 * chip + 1 - core]


def rows(chunks, last, ahead, table, occ, vir, highs, lows, integrals, got, total):
    size, count = integrals.shape[-1], len(chunks)
    used = [buffer for step in got[chunks[0] : chunks[-1] + 4] for buffer in step]
    first = total is None
    operands = (table, occ, vir, vir[:, None], vir[None, :], highs, lows, integrals, *used) + (() if first else (total,))
    specs = (SMEM, SMEM, SMEM, VMEM, VMEM, VMEM, VMEM) + (HBM,) * (1 + len(used)) + (() if first else (VMEM,))
    shape = (2 * PARTS, 2, size // (2 * PARTS), 3 * size)
    half = f32(PARTS, *shape[1:])
    fetched = () if ahead is None else (payload(integrals),) * 3
    scratch = (
        pltpu.VMEM((count, 3, ROWS, size, size), jnp.float32),
        pltpu.VMEM((count, 2, ROWS, size, size), jnp.float32),
        pltpu.SemaphoreType.DMA((count, 11)),
    )
    return call(
        lambda *refs: rows_kernel(chunks, first, last, ahead, *refs),
        (half, half) if last else (f32(*shape),) + fetched,
        operands,
        specs,
        (VMEM, VMEM) if last else (VMEM,) * (1 + len(fetched)),
        scratch + ((pltpu.VMEM(shape, jnp.float32),) if last else (pltpu.SemaphoreType.DMA((9,)),) if fetched else ()),
        cost=(count * ROWS * 72 * size**3, count * ROWS * 20 * size**2 + 12 * 6 * size**2),
        mib=51 if first else 46,
    )


def to_slabs_kernel(table_ref, amplitudes_ref, out_ref, sems):
    copies = []
    for n, (row, slab, q, slot, here) in enumerate(pairs_of(table_ref, (sems.shape[0] - 4) // 2, amplitudes_ref.shape[1])):
        copy = pltpu.make_async_copy(amplitudes_ref.at[row, q], out_ref.at[:, slot], sems.at[n])
        mine = here & (slab == table_ref[SLAB])
        pl.when(mine)(copy.start)
        copies.append((mine, copy))
    for mine, copy in copies:
        pl.when(mine)(copy.wait)


def to_groups_kernel(q_slab, table_ref, by_slab_ref, ki_ref, out_ref):
    groups = out_ref.shape[0]
    parts = [(slab, slot) for _, slab, _, slot, _ in pairs_of(table_ref, groups, q_slab)]
    for m in range(2):
        ki_ref[m] = by_slab_ref[parts[m]]
        value = by_slab_ref[parts[2 + m]]
        for g in range(groups):
            out_ref[g, m] = by_slab_ref[parts[4 + m * groups + g]]
            out_ref[g, 2 + m] = value


def my_pairs_kernel(table_ref, ki_ref, by_trip_ref, out_ref):
    size = ki_ref.shape[-1]
    for m in range(2):
        pairs = (by_trip_ref[table_ref[OWNER], 2 + m], by_trip_ref[table_ref[OWNER + 1 + m], m], ki_ref[m])
        for chip in range(out_ref.shape[0]):
            for n, value in enumerate(pairs):
                out_ref[chip, m, :, n * size : (n + 1) * size] = value


def split_kernel(table_ref, mine_ref, other_ref, high_ref, low_ref):
    size = high_ref.shape[-1]
    core = lax.rem(table_ref[SLAB], 2)
    half = mine_ref.shape[2]
    for m in range(2):
        for n in range(3):
            for chip in range(mine_ref.shape[0]):
                for ref, parity in ((mine_ref, core), (other_ref, 1 - core)):
                    start = pl.multiple_of((2 * chip + parity) * half, half)
                    high, low = split(ref[chip, m, :, n * size : (n + 1) * size])
                    high_ref[m, n, pl.ds(start, half)] = high
                    low_ref[m, n, pl.ds(start, half)] = low


def sums_kernel(in_ref, ki_ref, out_ref):
    size = ki_ref.shape[-1]
    sums = jnp.sum(in_ref[...], axis=0)
    ki_ref[...] = sums[:, :, 2 * size :]
    for g in range(out_ref.shape[0]):
        out_ref[g, :2] = sums[:, :, size : 2 * size]
        out_ref[g, 2:] = sums[:, :, :size]


def from_groups_kernel(q_slab, table_ref, ki_ref, arrived_ref, out_ref):
    groups = arrived_ref.shape[0]
    for n, (_, slab, _, slot, here) in enumerate(pairs_of(table_ref, groups, q_slab)):

        @pl.when(here)
        def _():
            if n < 2:
                value = ki_ref[n]
            elif n < 4:
                value = jnp.sum(arrived_ref[:, n], axis=0)
            else:
                m, g = divmod(n - 4, groups)
                value = arrived_ref[g, m]
            out_ref[slab, slot] = value


def result_kernel(groups, table_ref, in_ref, out_ref):
    out_ref[...] = jnp.zeros_like(out_ref)
    for row, slab, q, slot, here in pairs_of(table_ref, groups, out_ref.shape[1]):

        @pl.when(here & (slab == table_ref[SLAB]))
        def _():
            out_ref[row, q] += in_ref[:, slot]


def on_device(integrals, amplitudes, occ_energy, vir_energy, owner, triples):
    n_slab, n_trip = lax.axis_size("slab"), lax.axis_size("trip")
    rows_count, q_slab, size = amplitudes.shape[:3]
    part = size // n_slab
    same_core = [list(range(core, n_slab, 2)) for core in range(2)]
    other_core = [(slab, slab ^ 1) for slab in range(n_slab)]
    where = jnp.stack([lax.axis_index("trip"), lax.axis_index("slab")]).astype(jnp.int32)
    table = call(
        table_kernel,
        jax.ShapeDtypeStruct((TABLE,), jnp.int32),
        (owner, triples.reshape(-1), where),
        (SMEM,) * 3,
        SMEM,
        cost=(0, 1 << 10),
    )
    amplitudes = amplitudes.reshape(rows_count, q_slab, n_slab, part, size)
    slots = 2 * q_slab

    chunks = integrals.shape[1] // ROWS
    got, total, pairs, parts = [], None, None, None
    own = ()
    for step in range(chunks + 2):
        previous = tuple(got[-1]) if got else ()
        if step == 2:
            by_slab = lax.all_to_all(to_slabs, "slab", 0, 0, tiled=True)
            t_ki, to_groups = call(
                lambda *refs: to_groups_kernel(q_slab, *refs),
                (f32(2, part, size), f32(n_trip, 4, part, size)),
                (table, by_slab),
                (SMEM, VMEM),
                (VMEM, VMEM),
                cost=(0, 32 * n_trip * part * size),
            )
            t_ki, to_groups, *previous = lax.optimization_barrier((t_ki, to_groups, *previous))
        if step == 3:
            by_trip = lax.all_to_all(to_groups, "trip", 0, 0, tiled=True)
            by_trip, *previous = lax.optimization_barrier((by_trip, *previous))
        if total is not None:
            total, *previous = lax.optimization_barrier((total, *previous))
        sent = send(step if step <= chunks else None, table, integrals, previous, own)
        own = ()
        if step == 0:
            late_table, *sent = lax.optimization_barrier((table, *sent))
            to_slabs = call(
                to_slabs_kernel,
                f32(n_slab, slots, part, size),
                (late_table, amplitudes),
                (SMEM, HBM),
                VMEM,
                (pltpu.SemaphoreType.DMA((4 + 2 * n_trip,)),),
                cost=(0, 8 * slots * size**2),
            )
        if step == 3:
            by_trip, *sent = lax.optimization_barrier((by_trip, *sent))
            pairs = call(
                my_pairs_kernel,
                f32(PARTS, 2, part, 3 * size),
                (table, t_ki, by_trip),
                (SMEM, VMEM, VMEM),
                VMEM,
                cost=(0, 4 * 6 * size**2),
            )
            mine = lax.all_to_all(pairs, "slab", 0, 0, axis_index_groups=same_core, tiled=True)
        if step == 4:
            mine, *sent = lax.optimization_barrier((mine, *sent))
            other = lax.ppermute(mine, "slab", other_core)
            shape = jax.ShapeDtypeStruct((2, 3, size, size), jnp.bfloat16)
            parts = call(
                split_kernel,
                (shape, shape),
                (table, mine, other),
                (SMEM, VMEM, VMEM),
                (VMEM, VMEM),
                cost=(0, 16 * 6 * size**2),
            )
        got.append([lax.ppermute(sent[d], "trip", ALONG[d]) for d in range(3)])
        for key in (step,) if step < chunks + 1 else (step, step + 1):
            if key in WORK:
                last = key == chunks + 2
                ahead = step + 1 if step < chunks else None
                total, *own = rows(WORK[key], last, ahead, table, occ_energy, vir_energy, *parts, integrals, got, total)

    keep, give = total, *own
    give = lax.ppermute(give, "slab", other_core)
    by_slab = lax.all_to_all(keep + give, "slab", 0, 0, axis_index_groups=same_core, tiled=True)
    r_ki, outgoing = call(
        sums_kernel,
        (f32(2, part, size), f32(n_trip, 4, part, size)),
        (by_slab,),
        (VMEM,),
        (VMEM, VMEM),
    )
    arrived = lax.all_to_all(outgoing, "trip", 0, 0, tiled=True)
    to_slabs = call(
        lambda *refs: from_groups_kernel(q_slab, *refs),
        f32(n_slab, slots, part, size),
        (table, r_ki, arrived),
        (SMEM, VMEM, VMEM),
        VMEM,
    )
    result = call(
        lambda *refs: result_kernel(n_trip, *refs),
        f32(*amplitudes.shape),
        (table, lax.all_to_all(to_slabs, "slab", 0, 0, tiled=True)),
        (SMEM, VMEM),
        VMEM,
    )
    return result.reshape(rows_count, q_slab, size, size)


def solution(mesh):
    in_specs = (P("trip", "slab", None, None), P("trip", "slab", None, None), P(), P(), P(), P())
    out_specs = P("trip", "slab", None, None)
    return jax.shard_map(
        on_device, mesh=mesh, in_specs=in_specs, out_specs=out_specs, check_vma=False
    )
```

```python
import jax
import jax.numpy as jnp
from jax import lax
from jax.experimental import pallas as pl
from jax.experimental.pallas import tpu as pltpu
from jax.sharding import PartitionSpec as P

GRAY = (0, 1, 3, 2)
CUBE = tuple((t // 4) * 4 + GRAY[t % 4] for t in range(8))
FROM_CUBE = tuple(CUBE.index(v) for v in range(8))
ALONG = tuple([(t, FROM_CUBE[CUBE[t] ^ (1 << d)]) for t in range(8)] for d in range(3))

ARRIVE = [[None] * 8 for _ in range(3)]
FORWARD = [[0] * 8 for _ in range(3)]
for p in range(3):
    q, r = (p + 1) % 3, (p + 2) % 3
    a, b, c = 1 << p, 1 << q, 1 << r
    for node, depth, dim in ((a, 1, p), (a | b, 2, q), (a | c, 2, r), (7, 3, r), (b, 3, p), (c, 3, p), (b | c, 4, p)):
        ARRIVE[p][node] = (depth, dim)
    for node, dim in ((a, q), (a, r), (a | b, r), (a | b, p), (a | c, p), (7, p)):
        FORWARD[dim][node] = 1 + ARRIVE[p][node][1]
KINDS = [sorted(set(ARRIVE[p][1:])) for p in range(3)]
ARRIVAL = [[0] + [1 + KINDS[p].index(kind) for kind in ARRIVE[p][1:]] for p in range(3)]

PARTS = 8
ROWS = 2
WORK = {5: (0, 1), 6: (2,), 7: (3,), 8: (4,), 9: (5,), 10: (6, 7)}
PLACE, PLACE_K, SOURCE, ARRIVED, OWNER, OCC, OCC_K, ALL_K, TRIP, SLAB, TABLE = 0, 3, 5, 14, 23, 26, 29, 31, 47, 48, 49

HBM = pl.BlockSpec(memory_space=pltpu.HBM)
SMEM = pl.BlockSpec(memory_space=pltpu.SMEM)
VMEM = pl.BlockSpec(memory_space=pltpu.VMEM)


def pick(values, index):
    found = jnp.int32(values[0])
    for n in range(1, len(values)):
        found = jnp.where(index == n, jnp.int32(values[n]), found)
    return found


def call(kernel, out_shape, operands, specs, out_specs=None, scratch=(), mib=46, cost=(0, 1 << 20), aliases=None):
    return pl.pallas_call(
        kernel,
        in_specs=list(specs),
        out_specs=out_specs,
        out_shape=out_shape,
        scratch_shapes=list(scratch),
        input_output_aliases=aliases or {},
        cost_estimate=pl.CostEstimate(flops=cost[0], bytes_accessed=cost[1], transcendentals=0),
        compiler_params=pltpu.CompilerParams(vmem_limit_bytes=mib * 2**20),
    )(*operands)


def f32(*shape):
    return jax.ShapeDtypeStruct(shape, jnp.float32)


def table_kernel(owner_ref, triples_ref, where_ref, out_ref):
    count = owner_ref.shape[0]
    trip = where_ref[0]
    out_ref[TRIP], out_ref[SLAB] = trip, where_ref[1]
    groups = triples_ref.shape[0] // 6

    def triple(m, g, n):
        return triples_ref[(m * groups + g) * 3 + n]

    def rank(occ):
        mine = owner_ref[occ]
        total = jnp.int32(0)
        for other in range(count):
            total += ((other < occ) & (owner_ref[other] == mine)).astype(jnp.int32)
        return total

    for x, occ in enumerate((triple(0, 0, 0), triple(0, 0, 1), triple(1, 0, 1))):
        owner = owner_ref[occ]
        rho = pick(CUBE, trip) ^ pick(CUBE, owner)
        out_ref[PLACE + x], out_ref[OWNER + x], out_ref[OCC + x] = rank(occ), owner, occ
        for n in range(3):
            out_ref[SOURCE + 3 * x + n] = pick(FORWARD[n], rho)
            out_ref[ARRIVED + 3 * x + n] = pick(ARRIVAL[n], rho)
    for m in range(2):
        occ = triple(m, trip, 2)
        out_ref[PLACE_K + m], out_ref[OCC_K + m] = rank(occ), occ
        for g in range(groups):
            out_ref[ALL_K + m * groups + g] = triple(m, g, 2)


def pairs_of(table_ref, groups, q_slab):
    found = [(m, PLACE_K + m, OCC, None) for m in range(2)]
    found += [(m, PLACE, OCC + 1 + m, OWNER) for m in range(2)]
    found += [(m, PLACE + 1 + m, ALL_K + m * groups + g, OWNER + 1 + m) for m in range(2) for g in range(groups)]
    pairs = []
    for m, row, col, plane in found:
        slab, q = lax.div(table_ref[col], q_slab), lax.rem(table_ref[col], q_slab)
        here = True if plane is None else table_ref[plane] == table_ref[TRIP]
        pairs.append((table_ref[row], slab, q, m * q_slab + q, here))
    return pairs


def thirds(size):
    height = -(-size // 24) * 8
    return height, (0, height, size - height)


def own_part(integrals_ref, table_ref, x, chunk, p, low=0):
    height, offsets = thirds(integrals_ref.shape[2])
    return integrals_ref.at[
        table_ref[PLACE + x], pl.ds(chunk * ROWS, ROWS), pl.ds(offsets[p] + low, height - low), :
    ]


def fetch(table_ref, integrals_ref, step, targets, sems):
    chunk = min(step, integrals_ref.shape[1] // ROWS - 1)
    copies = []
    for d in range(3):
        for x in range(3):
            mine = pltpu.make_async_copy(
                own_part(integrals_ref, table_ref, x, chunk, (d + 2 * (step - chunk)) % 3), targets[d].at[x], sems.at[3 * d + x]
            )
            needed = table_ref[SOURCE + 3 * x + d] == 0
            pl.when(needed)(mine.start)
            copies.append((needed, mine))
    return copies


def send_kernel(step, n_got, n_own, table_ref, *refs):
    got, own, rest = refs[:n_got], refs[n_got : n_got + n_own], refs[n_got + n_own :]
    copies = []
    if step is not None and not own:
        integrals_ref, *sent, sems = rest
        copies = fetch(table_ref, integrals_ref, step, sent, sems)
    else:
        sent = rest
    for d in range(3):
        for x in range(3):
            source = table_ref[SOURCE + 3 * x + d]
            for e, ref in enumerate((*own[d : d + 1], *got)):

                @pl.when(source == e + 1 - len(own[d : d + 1]))
                def _():
                    sent[d][x] = got[e - len(own[d : d + 1])][x] if e >= len(own[d : d + 1]) else ref[x]

    for needed, copy in copies:
        pl.when(needed)(copy.wait)


def payload(integrals):
    size = integrals.shape[-1]
    return f32(3, ROWS, thirds(size)[0], size)


def send(step, table, integrals, got, own):
    shape = payload(integrals)
    reads = step is not None and not own
    return call(
        lambda *refs: send_kernel(step, len(got), len(own), *refs),
        (shape,) * 3,
        (table, *got, *own) + ((integrals,) if reads else ()),
        (SMEM,) + (VMEM,) * (len(got) + len(own)) + ((HBM,) if reads else ()),
        (VMEM,) * 3,
        (pltpu.SemaphoreType.DMA((9,)),) if reads else (),
        cost=(0, 6 * 4 * shape.size),
        mib=46 if got else 49,
    )


def split(value):
    high = value.astype(jnp.bfloat16)
    return high, (value - high.astype(jnp.float32)).astype(jnp.bfloat16)


def product(highs, lows, block, dims):
    size, count = highs[0].shape[0], len(highs)

    def dot(parts, right):
        left = parts[0] if len(parts) == 1 else jnp.concatenate(parts)
        return lax.dot_general(left, right, (dims, ((), ())), preferred_element_type=jnp.float32)

    both, rest = dot(highs + lows, block[0]), dot(highs, block[1])
    part = lambda value, n: value[n * size : (n + 1) * size]
    return [part(both, n) + part(both, count + n) + part(rest, n) for n in range(count)]


def rows_kernel(chunks, first, last, ahead, table_ref, occ_ref, vir_c_ref, vir_a_ref, vir_b_ref, high_ref, low_ref, integrals_ref, *refs):
    count = 3 * (len(chunks) + (2 if last else 3))
    got, rest = refs[:count], refs[count:]
    if not first:
        in_ref, rest = rest[0], rest[1:]
    if last:
        keep_ref, give_ref, w_ref, k_ref, sems, out_ref = rest
    else:
        out_ref, rest = rest[0], rest[1:]
        if ahead is not None:
            own, own_sems, rest = rest[:3], rest[-1], rest[3:-1]
        w_ref, k_ref, sems = rest
    size = w_ref.shape[-1]
    height, offsets = thirds(size)

    copies = []
    for n, chunk in enumerate(chunks):
        for m in range(2):
            source = integrals_ref.at[table_ref[PLACE_K + m], pl.ds(chunk * ROWS, ROWS)]
            mine = pltpu.make_async_copy(source, k_ref.at[n, m], sems.at[n, 9 + m])
            mine.start()
            copies.append(mine)
        for x in range(3):
            for p in range(3):
                low = offsets[1] + height - offsets[2] if p == 2 else 0
                target = w_ref.at[n, x, :, pl.ds(offsets[p] + low, height - low), :]
                sem = sems.at[n, 3 * x + p]
                arrived = table_ref[ARRIVED + 3 * x + p]
                mine = pltpu.make_async_copy(own_part(integrals_ref, table_ref, x, chunk, p, low), target, sem)
                pl.when(arrived == 0)(mine.start)
                for kind, (depth, dim) in enumerate(KINDS[p]):
                    if depth == 4 and last and n == len(chunks) - 1:
                        depth, dim = 3, (p + 2) % 3
                    source = got[3 * (n + depth - 1) + dim].at[x, :, pl.ds(low, height - low), :]
                    pl.when(arrived == 1 + kind)(pltpu.make_async_copy(source, target, sem).start)
                copies.append(mine)
    own_copies = [] if ahead is None else fetch(table_ref, integrals_ref, ahead, own, own_sems)
    out_ref[...] = jnp.zeros_like(out_ref) if first else in_ref[...]
    virs = vir_a_ref[...] + vir_b_ref[...]
    shift_ij = [occ_ref[table_ref[OCC]] + occ_ref[table_ref[OCC + 1 + m]] for m in range(2)]
    shifts = [shift_ij[m] + occ_ref[table_ref[OCC_K + m]] for m in range(2)]
    for copy in copies:
        copy.wait()

    @pl.loop(0, len(chunks) * ROWS, unroll=True)
    def _(step):
        n, row = lax.div(step, ROWS), lax.rem(step, ROWS)
        c = table_ref[SLAB] * integrals_ref.shape[1] + chunks[0] * ROWS + step
        shared = [split(w_ref[n, x, row]) for x in range(3)]
        blocks = [[split(k_ref[n, m, row]) for m in range(2)], [shared[0]], [shared[1], shared[2]]]

        def against(highs, lows, dims):
            found = []
            for b in range(3):
                if len(blocks[b]) == 1:
                    found.append(product([highs(m, b) for m in range(2)], [lows(m, b) for m in range(2)], blocks[b][0], dims))
                else:
                    found.append([product([highs(m, b)], [lows(m, b)], blocks[b][m], dims)[0] for m in range(2)])
            return found

        terms = against(lambda m, b: high_ref[m, b], lambda m, b: low_ref[m, b], ((1,), (0,)))
        amps = []
        for m in range(2):
            connected = terms[0][m] + terms[1][m] + terms[2][m]
            amps.append(split(connected / (shifts[m] - (virs + vir_c_ref[c]))))
        terms = against(lambda m, b: amps[m][0], lambda m, b: amps[m][1], ((1,), (1,)))
        for m in range(2):
            for b in range(3):
                out_ref[:, m, :, b * size : (b + 1) * size] += terms[b][m].reshape(out_ref.shape[0], -1, size)

    for needed, copy in own_copies:
        pl.when(needed)(copy.wait)
    if last:
        core = lax.rem(table_ref[SLAB], 2)
        for chip in range(keep_ref.shape[0]):
            keep_ref[chip] = out_ref[2 * chip + core]
            give_ref[chip] = out_ref[2 * chip + 1 - core]


def rows(chunks, last, ahead, table, occ, vir, highs, lows, integrals, got, total):
    size, count = integrals.shape[-1], len(chunks)
    used = [buffer for step in got[chunks[0] : chunks[-1] + 4] for buffer in step]
    first = total is None
    operands = (table, occ, vir, vir[:, None], vir[None, :], highs, lows, integrals, *used) + (() if first else (total,))
    specs = (SMEM, SMEM, SMEM, VMEM, VMEM, VMEM, VMEM) + (HBM,) * (1 + len(used)) + (() if first else (VMEM,))
    shape = (2 * PARTS, 2, size // (2 * PARTS), 3 * size)
    half = f32(PARTS, *shape[1:])
    fetched = () if ahead is None else (payload(integrals),) * 3
    scratch = (
        pltpu.VMEM((count, 3, ROWS, size, size), jnp.float32),
        pltpu.VMEM((count, 2, ROWS, size, size), jnp.float32),
        pltpu.SemaphoreType.DMA((count, 11)),
    )
    return call(
        lambda *refs: rows_kernel(chunks, first, last, ahead, *refs),
        (half, half) if last else (f32(*shape),) + fetched,
        operands,
        specs,
        (VMEM, VMEM) if last else (VMEM,) * (1 + len(fetched)),
        scratch + ((pltpu.VMEM(shape, jnp.float32),) if last else (pltpu.SemaphoreType.DMA((9,)),) if fetched else ()),
        cost=(count * ROWS * 72 * size**3, count * ROWS * 20 * size**2 + 12 * 6 * size**2),
        mib=51 if first else 46,
    )


def to_slabs_kernel(table_ref, amplitudes_ref, out_ref, sems):
    copies = []
    for n, (row, slab, q, slot, here) in enumerate(pairs_of(table_ref, (sems.shape[0] - 4) // 2, amplitudes_ref.shape[1])):
        copy = pltpu.make_async_copy(amplitudes_ref.at[row, q], out_ref.at[:, slot], sems.at[n])
        mine = here & (slab == table_ref[SLAB])
        pl.when(mine)(copy.start)
        copies.append((mine, copy))
    for mine, copy in copies:
        pl.when(mine)(copy.wait)


def to_groups_kernel(q_slab, table_ref, by_slab_ref, ki_ref, out_ref):
    groups = out_ref.shape[0]
    parts = [(slab, slot) for _, slab, _, slot, _ in pairs_of(table_ref, groups, q_slab)]
    for m in range(2):
        ki_ref[m] = by_slab_ref[parts[m]]
        value = by_slab_ref[parts[2 + m]]
        for g in range(groups):
            out_ref[g, m] = by_slab_ref[parts[4 + m * groups + g]]
            out_ref[g, 2 + m] = value


def my_pairs_kernel(table_ref, ki_ref, by_trip_ref, out_ref):
    size = ki_ref.shape[-1]
    for m in range(2):
        pairs = (by_trip_ref[table_ref[OWNER], 2 + m], by_trip_ref[table_ref[OWNER + 1 + m], m], ki_ref[m])
        for chip in range(out_ref.shape[0]):
            for n, value in enumerate(pairs):
                out_ref[chip, m, :, n * size : (n + 1) * size] = value


def split_kernel(table_ref, mine_ref, other_ref, high_ref, low_ref):
    size = high_ref.shape[-1]
    core = lax.rem(table_ref[SLAB], 2)
    half = mine_ref.shape[2]
    for m in range(2):
        for n in range(3):
            for chip in range(mine_ref.shape[0]):
                for ref, parity in ((mine_ref, core), (other_ref, 1 - core)):
                    start = pl.multiple_of((2 * chip + parity) * half, half)
                    high, low = split(ref[chip, m, :, n * size : (n + 1) * size])
                    high_ref[m, n, pl.ds(start, half)] = high
                    low_ref[m, n, pl.ds(start, half)] = low


def sums_kernel(in_ref, ki_ref, out_ref):
    size = ki_ref.shape[-1]
    sums = jnp.sum(in_ref[...], axis=0)
    ki_ref[...] = sums[:, :, 2 * size :]
    for g in range(out_ref.shape[0]):
        out_ref[g, :2] = sums[:, :, size : 2 * size]
        out_ref[g, 2:] = sums[:, :, :size]


def from_groups_kernel(q_slab, table_ref, ki_ref, arrived_ref, out_ref):
    groups = arrived_ref.shape[0]
    for n, (_, slab, _, slot, here) in enumerate(pairs_of(table_ref, groups, q_slab)):

        @pl.when(here)
        def _():
            if n < 2:
                value = ki_ref[n]
            elif n < 4:
                value = jnp.sum(arrived_ref[:, n], axis=0)
            else:
                m, g = divmod(n - 4, groups)
                value = arrived_ref[g, m]
            out_ref[slab, slot] = value


def result_kernel(groups, table_ref, in_ref, out_ref):
    out_ref[...] = jnp.zeros_like(out_ref)
    for row, slab, q, slot, here in pairs_of(table_ref, groups, out_ref.shape[1]):

        @pl.when(here & (slab == table_ref[SLAB]))
        def _():
            out_ref[row, q] += in_ref[:, slot]


def on_device(integrals, amplitudes, occ_energy, vir_energy, owner, triples):
    n_slab, n_trip = lax.axis_size("slab"), lax.axis_size("trip")
    rows_count, q_slab, size = amplitudes.shape[:3]
    part = size // n_slab
    same_core = [list(range(core, n_slab, 2)) for core in range(2)]
    other_core = [(slab, slab ^ 1) for slab in range(n_slab)]
    where = jnp.stack([lax.axis_index("trip"), lax.axis_index("slab")]).astype(jnp.int32)
    table = call(
        table_kernel,
        jax.ShapeDtypeStruct((TABLE,), jnp.int32),
        (owner, triples.reshape(-1), where),
        (SMEM,) * 3,
        SMEM,
        cost=(0, 1 << 10),
    )
    amplitudes = amplitudes.reshape(rows_count, q_slab, n_slab, part, size)
    slots = 2 * q_slab

    chunks = integrals.shape[1] // ROWS
    got, total, pairs, parts = [], None, None, None
    own = ()
    for step in range(chunks + 2):
        previous = tuple(got[-1]) if got else ()
        if step == 2:
            by_slab = lax.all_to_all(to_slabs, "slab", 0, 0, tiled=True)
            t_ki, to_groups = call(
                lambda *refs: to_groups_kernel(q_slab, *refs),
                (f32(2, part, size), f32(n_trip, 4, part, size)),
                (table, by_slab),
                (SMEM, VMEM),
                (VMEM, VMEM),
                cost=(0, 32 * n_trip * part * size),
            )
            t_ki, to_groups, *previous = lax.optimization_barrier((t_ki, to_groups, *previous))
        if step == 3:
            by_trip = lax.all_to_all(to_groups, "trip", 0, 0, tiled=True)
            by_trip, *previous = lax.optimization_barrier((by_trip, *previous))
        if total is not None:
            total, *previous = lax.optimization_barrier((total, *previous))
        sent = send(step if step <= chunks else None, table, integrals, previous, own)
        own = ()
        if step == 0:
            late_table, *sent = lax.optimization_barrier((table, *sent))
            to_slabs = call(
                to_slabs_kernel,
                f32(n_slab, slots, part, size),
                (late_table, amplitudes),
                (SMEM, HBM),
                VMEM,
                (pltpu.SemaphoreType.DMA((4 + 2 * n_trip,)),),
                cost=(0, 8 * slots * size**2),
            )
        if step == 3:
            by_trip, *sent = lax.optimization_barrier((by_trip, *sent))
            pairs = call(
                my_pairs_kernel,
                f32(PARTS, 2, part, 3 * size),
                (table, t_ki, by_trip),
                (SMEM, VMEM, VMEM),
                VMEM,
                cost=(0, 4 * 6 * size**2),
            )
            mine = lax.all_to_all(pairs, "slab", 0, 0, axis_index_groups=same_core, tiled=True)
        if step == 4:
            mine, *sent = lax.optimization_barrier((mine, *sent))
            other = lax.ppermute(mine, "slab", other_core)
            shape = jax.ShapeDtypeStruct((2, 3, size, size), jnp.bfloat16)
            parts = call(
                split_kernel,
                (shape, shape),
                (table, mine, other),
                (SMEM, VMEM, VMEM),
                (VMEM, VMEM),
                cost=(0, 16 * 6 * size**2),
            )
        got.append([lax.ppermute(sent[d], "trip", ALONG[d]) for d in range(3)])
        for key in (step,) if step < chunks + 1 else (step, step + 1):
            if key in WORK:
                last = key == chunks + 2
                ahead = step + 1 if step < chunks else None
                total, *own = rows(WORK[key], last, ahead, table, occ_energy, vir_energy, *parts, integrals, got, total)

    keep, give = total, *own
    give = lax.ppermute(give, "slab", other_core)
    by_slab = lax.all_to_all(keep + give, "slab", 0, 0, axis_index_groups=same_core, tiled=True)
    r_ki, outgoing = call(
        sums_kernel,
        (f32(2, part, size), f32(n_trip, 4, part, size)),
        (by_slab,),
        (VMEM,),
        (VMEM, VMEM),
    )
    arrived = lax.all_to_all(outgoing, "trip", 0, 0, tiled=True)
    to_slabs = call(
        lambda *refs: from_groups_kernel(q_slab, *refs),
        f32(n_slab, slots, part, size),
        (table, r_ki, arrived),
        (SMEM, VMEM, VMEM),
        VMEM,
    )
    result = call(
        lambda *refs: result_kernel(n_trip, *refs),
        f32(*amplitudes.shape),
        (table, lax.all_to_all(to_slabs, "slab", 0, 0, tiled=True)),
        (SMEM, VMEM),
        VMEM,
    )
    return result.reshape(rows_count, q_slab, size, size)


def solution(mesh):
    in_specs = (P("trip", "slab", None, None), P("trip", "slab", None, None), P(), P(), P(), P())
    out_specs = P("trip", "slab", None, None)
    return jax.shard_map(
        on_device, mesh=mesh, in_specs=in_specs, out_specs=out_specs, check_vma=False
    )
```
